512 devices in a mesh: dp: 64 (over y, z), group: 8 (over x, core).
Axes of the slice: x: 4, y: 4, z: 16, core: 2. Of those that a mesh axis runs over, the one named last changes fastest.
Arguments:
- queries: bfloat16 [8, 8192, 4096], P('group', 'dp'), may hold values from -6 to 6
- out_grad: bfloat16 [8, 8192, 4096], P('group', 'dp')
- keys_values: bfloat16 [8, 8192, 1024], P('group', 'dp'), may hold values from -6 to 6
- prompt_kv: bfloat16 [8, 4096, 1024], P('group', 'dp'), may hold values from -6 to 6
- q_gain: float32 [128], replicated, may hold values from 0.5 to 1.5
- k_gain: float32 [128], replicated, may hold values from 0.5 to 1.5
- block_owner: int32 [8, 128], P('group', 'dp'), may hold values from 0 to 63, as said below
- block_start: int32 [8, 128], P('group', 'dp'), may hold values 0 or 1
Outputs:
- query_grad: bfloat16 [8, 8192, 4096], P('group', 'dp')
- kv_grad: bfloat16 [8, 8192, 1024], P('group', 'dp')
- prompt_kv_grad: bfloat16 [8, 4096, 1024], P('group', 'dp')
- gain_grads: float32 [2, 128], replicated
The draws below stay inside these ranges and needn't reach their ends.
Inputs may be any that keep to these rules, and one draw needn't show every extreme that they name: Within a group block_owner never falls from one block to the next; block i (on device i // 2) names a prompt between i // 2 - (3) and i // 2, and in every group some block names the prompt exactly 3 devices before its own.
All inputs are finite; a program needn't handle non-finite values. No bound on the sum of `block_start` on one device may be relied on, other than what follows from the above.
Results may differ from the reference program's by a relative error of at most 0.01.
Values may be sent and summed in bfloat16 or wider, within the bound.
A program may use at most 64 MiB of HBM per device.

```python
import math
import jax
import jax.numpy as jnp
from jax import lax

H = 32
KVH = 4
HD = 128
BLK = 64
NB = 2
SPAN = 4
P_SIZE = 64
QW = 4096
KW = 512
CT = 128
ROWS = 8192
PROWS = 4096
BLOCKS = 128
GROUPS = 8


def draw_out_grad(key, part):
    key = jax.random.fold_in(key, 5)
    per_group = ROWS // CT
    count = max(GROUPS * per_group - 1, 1)
    position = jnp.arange(GROUPS)[:, None] * per_group + jnp.arange(ROWS)[None, :] // CT
    ranking = position.astype(jnp.float32) / count
    noise = jax.random.normal(key, (GROUPS, ROWS, QW), jnp.float32)
    factor = 4.0 + 8.0 * ranking
    return (noise * factor[:, :, None]).astype(jnp.bfloat16)


def draw_block_owner(key, part):
    key = jax.random.fold_in(key, 11)
    first_key, second_key = jax.random.split(key)
    limit = NB * (SPAN - 1)
    lags = jax.random.randint(first_key, (GROUPS, BLOCKS), 0, limit + 1)
    anchor = jax.random.randint(second_key, (GROUPS, 1), limit, BLOCKS)
    block_index = jnp.arange(BLOCKS, dtype=jnp.int32)[None, :]
    forced = (block_index >= anchor - limit) & (block_index <= anchor)
    lags = jnp.where(forced, limit, lags)
    leading = lax.cummax(block_index - lags, axis=1)
    return (jnp.maximum(leading, 0) // NB).astype(jnp.int32)


def touch_ends(entries, own_key, smallest, high):
    index_at = [jax.random.randint(jax.random.fold_in(own_key, axis), (), 0, length) for axis, length in enumerate(entries.shape)]
    widest = entries.shape.index(max(entries.shape))
    next_to = index_at[:widest] + [(index_at[widest] + 1) % entries.shape[widest]] + index_at[widest + 1:]
    return entries.at[tuple(index_at)].set(smallest).at[tuple(next_to)].set(high)


def level_of(stream_key, extent, pieces, least, high):
    level = 1.0
    for dim, shards_of in pieces:
        draws = jax.random.uniform(jax.random.fold_in(jax.random.fold_in(stream_key, 6), dim), (shards_of,), jnp.float32, least / len(pieces), high / len(pieces))
        level = level * jnp.repeat(jnp.exp(draws), extent[dim] // shards_of).reshape((-1,) + (1,) * (len(extent) - 1 - dim))
    return level


def centred(key, dims, scale, reach, cuts=(), kind=jnp.bfloat16):
    drawn = scale * jax.random.normal(key, dims, jnp.float32)
    if cuts:
        drawn = drawn * level_of(key, dims, cuts, -0.22, 0.18)
    return jnp.clip(drawn, -reach, reach).astype(kind)


def setup_inputs(seed: int = 0) -> dict:
    seeds = jax.random.split(jax.random.key(seed), 9)
    return {
        "queries": centred(seeds[0], (GROUPS, ROWS, QW), 1.0, 6.0, ((0, 8), (1, 64))),
        "out_grad": draw_out_grad(jax.random.fold_in(seeds[8], 71), 0),
        "keys_values": centred(seeds[2], (GROUPS, ROWS, 2 * KW), 1.0, 6.0, ((0, 8), (1, 64))),
        "prompt_kv": centred(seeds[3], (GROUPS, PROWS, 2 * KW), 1.0, 6.0, ((0, 8), (1, 64))),
        "q_gain": jnp.clip(1.0 + 0.1 * jax.random.normal(seeds[4], (HD,), jnp.float32), 0.5, 1.5),
        "k_gain": jnp.clip(1.0 + 0.1 * jax.random.normal(seeds[5], (HD,), jnp.float32), 0.5, 1.5),
        "block_owner": draw_block_owner(jax.random.fold_in(seeds[8], 71), 0),
        "block_start": touch_ends((jax.random.randint(seeds[7], (GROUPS, BLOCKS), 0, 3) < 1).astype(jnp.int32), jax.random.fold_in(seeds[7], 1), 0, 1),
    }


NORM_EPS = 1e-06

def rounded(values):
    return lax.optimization_barrier(values.astype(jnp.bfloat16)).astype(jnp.float32)

def unit_rows(raw_rows):
    return raw_rows * lax.rsqrt(lax.optimization_barrier(jnp.mean(raw_rows * raw_rows, axis=-1, keepdims=True)) + NORM_EPS)

def norm_backward(raw_rows, gain_vector, upstream):
    inverse = lax.rsqrt(lax.optimization_barrier(jnp.mean(raw_rows * raw_rows, axis=-1, keepdims=True)) + NORM_EPS)
    weighted = upstream * gain_vector
    d_raw = inverse * weighted - raw_rows * inverse ** 3 * lax.optimization_barrier(jnp.mean(raw_rows * weighted, axis=-1, keepdims=True))
    d_gain = lax.optimization_barrier(jnp.sum((raw_rows * inverse * upstream).reshape(-1, raw_rows.shape[-1]), axis=0))
    return (d_raw, d_gain)

def row_segments(owners, starts):
    changed = jnp.concatenate([jnp.ones((1,), jnp.int32), jnp.maximum(starts[1:], (owners[1:] != owners[:-1]).astype(jnp.int32))])
    return jnp.repeat(jnp.cumsum(changed).astype(jnp.int32), BLK, total_repeat_length=NB * BLK)

def device_terms(queries, out_grad, keys_values, prefix, segments, q_gain, k_gain):
    members = H // KVH
    score_scale = HD ** (-0.5)
    q_raw = queries.astype(jnp.float32).reshape(CT, KVH, members, HD)
    q_norm = rounded(unit_rows(q_raw) * q_gain)
    k_raw = keys_values[:, :KW].astype(jnp.float32).reshape(CT, KVH, HD)
    k_norm = rounded(unit_rows(k_raw) * k_gain)
    values = keys_values[:, KW:].astype(jnp.float32).reshape(CT, KVH, HD)
    p_raw = prefix[:, :, :KW].astype(jnp.float32).reshape(NB, P_SIZE, KVH, HD)
    p_norm = rounded(unit_rows(p_raw) * k_gain)
    p_values = prefix[:, :, KW:].astype(jnp.float32).reshape(NB, P_SIZE, KVH, HD)
    key_all = jnp.concatenate([jnp.broadcast_to(k_norm[None], (NB, CT, KVH, HD)), p_norm], axis=1)
    value_all = jnp.concatenate([jnp.broadcast_to(values[None], (NB, CT, KVH, HD)), p_values], axis=1)
    q_blocks = q_norm.reshape(NB, BLK, KVH, members, HD)
    out_blocks = out_grad.astype(jnp.float32).reshape(NB, BLK, KVH, members, HD)
    scores = jnp.einsum('nbkgd,nskd->nkgbs', q_blocks, key_all) * score_scale
    row_index = jnp.arange(CT, dtype=jnp.int32).reshape(NB, BLK)
    column = jnp.arange(CT + P_SIZE, dtype=jnp.int32)
    seg_cols = jnp.concatenate([segments, jnp.full((P_SIZE,), -1, jnp.int32)])
    seg_rows = segments.reshape(NB, BLK)
    allowed = (column[None, None, :] >= CT) | (seg_rows[:, :, None] == seg_cols[None, None, :]) & (column[None, None, :] <= row_index[:, :, None])
    exps = jnp.where(allowed[:, None, None, :, :], jnp.exp(scores), 0.0)
    totals = lax.optimization_barrier(jnp.sum(exps, axis=-1, keepdims=True))
    prob = exps / totals
    weight = rounded(prob)
    attended = jnp.einsum('nkgbs,nskd->nbkgd', weight, value_all)
    delta = lax.optimization_barrier(jnp.sum(out_blocks * attended, axis=-1)).transpose(0, 2, 3, 1)
    d_prob = jnp.einsum('nbkgd,nskd->nkgbs', out_blocks, value_all)
    d_score = rounded(prob * (d_prob - delta[..., None]))
    d_qnorm = jnp.einsum('nkgbs,nskd->nbkgd', d_score, key_all).reshape(CT, KVH, members, HD) * score_scale
    d_key_all = jnp.einsum('nkgbs,nbkgd->nskd', d_score, q_blocks) * score_scale
    d_value_all = jnp.einsum('nkgbs,nbkgd->nskd', weight, out_blocks)
    d_knorm = lax.optimization_barrier(jnp.sum(d_key_all[:, :CT], axis=0))
    d_values = lax.optimization_barrier(jnp.sum(d_value_all[:, :CT], axis=0))
    d_pnorm = d_key_all[:, CT:]
    d_pvalues = d_value_all[:, CT:]
    d_query, q_part = norm_backward(q_raw, q_gain, d_qnorm)
    d_key, k_part = norm_backward(k_raw, k_gain, d_knorm)
    query_grad = d_query.reshape(CT, QW).astype(jnp.bfloat16)
    kv_grad = jnp.concatenate([d_key.reshape(CT, KW), d_values.reshape(CT, KW)], axis=1).astype(jnp.bfloat16)
    prefix_part = jnp.concatenate([d_pnorm.reshape(NB, P_SIZE, KW), d_pvalues.reshape(NB, P_SIZE, KW)], axis=-1)
    return (query_grad, kv_grad, prefix_part, q_part, k_part)

def reference(queries, out_grad, keys_values, prompt_kv, q_gain, k_gain, block_owner, block_start):
    groups = queries.shape[0]
    devices = ROWS // CT
    prompt_all = prompt_kv.reshape(groups, devices, P_SIZE, 2 * KW)

    def one_device(carried, device_index):
        prompt_sums, gain_sums = carried
        group_index = device_index // devices
        local_index = device_index % devices
        zero = jnp.zeros((), jnp.int32)
        rows_q = lax.dynamic_slice(queries, (group_index, local_index * CT, zero), (1, CT, QW))[0]
        rows_g = lax.dynamic_slice(out_grad, (group_index, local_index * CT, zero), (1, CT, QW))[0]
        rows_kv = lax.dynamic_slice(keys_values, (group_index, local_index * CT, zero), (1, CT, 2 * KW))[0]
        owners = lax.dynamic_slice(block_owner, (group_index, local_index * NB), (1, NB))[0]
        starts = lax.dynamic_slice(block_start, (group_index, local_index * NB), (1, NB))[0]
        prefix = prompt_all[group_index][owners]
        segments = row_segments(owners, starts)
        query_grad, kv_grad, prefix_part, q_part, k_part = device_terms(rows_q, rows_g, rows_kv, prefix, segments, q_gain, k_gain)
        prompt_sums = prompt_sums.at[group_index, owners].add(prefix_part)
        gain_sums = gain_sums + jnp.stack([q_part, k_part])
        return ((prompt_sums, gain_sums), (query_grad, kv_grad))
    start_state = (jnp.zeros((groups, devices, P_SIZE, 2 * KW), jnp.float32), jnp.zeros((2, HD), jnp.float32))
    (prompt_sums, gain_sums), (query_rows, kv_rows) = lax.scan(one_device, start_state, jnp.arange(groups * devices, dtype=jnp.int32))
    prompt_raw = prompt_all[:, :, :, :KW].astype(jnp.float32).reshape(groups, devices, P_SIZE, KVH, HD)
    d_prompt_key, prompt_gain_part = norm_backward(prompt_raw, k_gain, prompt_sums[:, :, :, :KW].reshape(groups, devices, P_SIZE, KVH, HD))
    prompt_kv_grad = jnp.concatenate([d_prompt_key.reshape(groups, devices, P_SIZE, KW), prompt_sums[:, :, :, KW:]], axis=-1).astype(jnp.bfloat16).reshape(groups, devices * P_SIZE, 2 * KW)
    gain_sums = gain_sums + jnp.stack([jnp.zeros((HD,), jnp.float32), prompt_gain_part])
    gain_grads = gain_sums * (1.0 / math.sqrt(groups * ROWS))
    query_grad = query_rows.reshape(groups, ROWS, QW)
    kv_grad = kv_rows.reshape(groups, ROWS, 2 * KW)
    return (query_grad, kv_grad, prompt_kv_grad, gain_grads)
```

```python
import functools
import math

import jax
import jax.numpy as jnp
from jax import lax
from jax.experimental import pallas as pl
from jax.experimental.pallas import tpu as pltpu
from jax.sharding import PartitionSpec as P

H = 32
KVH = 4
HD = 128
BLK = 64
SPAN = 4
P_SIZE = 64
QW = 4096
KW = 512
CT = 128
MEMBERS = H // KVH
ROWS = MEMBERS * BLK
NORM_EPS = 1e-06
SCALE = HD**-0.5
LOG2E = math.log2(math.e)
ZS = 16
YS = 4
GS = 8
F32 = jnp.float32
BF16 = jnp.bfloat16
MESH = pl.DeviceIdType.MESH


def nt(a, b):
    return lax.dot_general(a, b, (((1,), (1,)), ((), ())), preferred_element_type=F32)


def nn(a, b):
    return jnp.dot(a, b, preferred_element_type=F32)


def tn(a, b):
    return lax.dot_general(a, b, (((0,), (0,)), ((), ())), preferred_element_type=F32)


def fold8(a):
    return jnp.sum(a.reshape(a.shape[0] // 8, 8, a.shape[1]), axis=0)


def unit_factor(raw):
    return lax.rsqrt(jnp.mean(raw * raw, axis=-1, keepdims=True) + NORM_EPS)


def norm_backward(raw, inverse, weighted):
    return inverse * weighted - raw * (inverse * inverse * inverse) * jnp.mean(
        raw * weighted, axis=-1, keepdims=True
    )


def kernel(
    q_hbm, g_hbm, kv_hbm, p_hbm, qgain, kgain, owner, start,
    qg_hbm, kvg_hbm, pg_hbm, gains_ref,
    q_v, g_v, kv_v, p_v, qg_v, kvg_v, pg_v, cand, parts, gsend, grecv, ar1, ar2, ar3,
    q_sem, g_sem, kv_sem, p_sem, out_sem, f_send, f_recv, b_send, b_recv,
    a1_send, a1_recv, a2_send, a2_recv, a3_send, a3_recv,
):
    me = lax.axis_index("dp")
    grp = lax.axis_index("group")
    right, left = lax.rem(me + 1, ZS * YS), lax.rem(me + ZS * YS - 1, ZS * YS)
    my_y, my_z = me // ZS, lax.rem(me, ZS)

    def group_peer(j):
        return (me, lax.rem(grp + j, GS))

    def y_peer(j):
        return (lax.rem(my_y + j, YS) * ZS + my_z, grp)

    def z_peer(j):
        return (my_y * ZS + lax.rem(my_z + j, ZS), grp)

    p_load = pltpu.make_async_copy(p_hbm.at[0], p_v, p_sem)
    p_load.start()
    kv_load = pltpu.make_async_copy(kv_hbm.at[0], kv_v, kv_sem)
    kv_load.start()
    q_loads, g_loads = [], []
    for h in range(KVH):
        cols = pl.ds(h * MEMBERS * HD, MEMBERS * HD)
        q_loads.append(pltpu.make_async_copy(q_hbm.at[0, :, cols], q_v.at[:, cols], q_sem.at[h]))
        g_loads.append(pltpu.make_async_copy(g_hbm.at[0, :, cols], g_v.at[:, cols], g_sem.at[h]))
        q_loads[h].start()
        g_loads[h].start()

    barrier = pltpu.get_barrier_semaphore()
    partners = [(right, grp), (left, grp)]
    partners += [group_peer(j) for j in range(1, GS)]
    partners += [y_peer(j) for j in range(1, YS)]
    partners += [z_peer(j) for j in range(1, ZS)]
    for peer in partners:
        pl.semaphore_signal(barrier, inc=1, device_id=peer, device_id_type=MESH)
    pl.semaphore_wait(barrier, len(partners))

    def hop(k, h):
        copies = []
        for part in range(2):
            if k == 0:
                src = p_hbm.at[0, :, pl.ds(part * KW + h * HD, HD)]
            else:
                src = cand.at[k - 1, h, part]
            copies.append(
                pltpu.make_async_remote_copy(
                    src_ref=src,
                    dst_ref=cand.at[k, h, part],
                    send_sem=f_send.at[k, h, part],
                    recv_sem=f_recv.at[k, h, part],
                    device_id=(right, grp),
                    device_id_type=MESH,
                )
            )
        return copies

    def send(k, h):
        for copy in hop(k, h):
            copy.start()

    def arrive(k, h):
        for copy in hop(k, h):
            copy.wait_recv()

    def pump(k, h):
        arrive(k - 1, h)
        send(k, h)

    def back(k, h):
        return pltpu.make_async_remote_copy(
            src_ref=gsend.at[k, h],
            dst_ref=grecv.at[k, h],
            send_sem=b_send.at[k, h],
            recv_sem=b_recv.at[k, h],
            device_id=(left, grp),
            device_id_type=MESH,
        )

    def back_step(k, h):
        back(k + 1, h).wait_recv()
        gsend[k, h] = (parts[k + 1, h] + grecv[k + 1, h].astype(F32)).astype(BF16)
        back(k, h).start()

    send(0, 0)
    send(0, 1)

    cq = qgain[...]
    ck = kgain[...]
    cqk = cq * ck
    slot0 = me - owner[0, 0]
    slot1 = me - owner[0, 1]
    same = jnp.where((start[0, 1] == 1) | (owner[0, 0] != owner[0, 1]), 0.0, 1.0).astype(F32)
    key_at = lax.broadcasted_iota(jnp.int32, (BLK, ROWS), 0)
    row_at = lax.rem(lax.broadcasted_iota(jnp.int32, (BLK, ROWS), 1), BLK)
    tri = key_at <= row_at
    ones8 = jnp.ones((8, HD), BF16)
    sub16 = lax.broadcasted_iota(jnp.int32, (16, ROWS), 0)
    wide16 = jnp.concatenate(
        [jnp.zeros((16, HD), BF16), jnp.where(lax.broadcasted_iota(jnp.int32, (16, HD), 0) < 2, 1.0, 0.0).astype(BF16)],
        axis=1,
    )

    def rows_of(ref, n, h):
        return jnp.concatenate(
            [
                ref[n * BLK : (n + 1) * BLK, (h * MEMBERS + m) * HD : (h * MEMBERS + m + 1) * HD]
                for m in range(MEMBERS)
            ],
            axis=0,
        )

    def attend(n, h, keys, vals):
        count = keys.shape[0]
        x = rows_of(q_v, n, h)
        g = rows_of(g_v, n, h)
        s = lax.rsqrt(nt(ones8, x * x)[0:1] * (1.0 / HD) + NORM_EPS)
        raw = nt(keys, x)
        e = jnp.exp2(raw * (s * (SCALE * LOG2E)))
        if n == 0:
            e = jnp.concatenate([jnp.where(tri, e[:BLK], 0.0), e[BLK:]], axis=0)
        else:
            e = jnp.concatenate(
                [e[:BLK] * same, jnp.where(tri, e[BLK : 2 * BLK], 0.0), e[2 * BLK :]], axis=0
            )
        prob = e * (1.0 / jnp.sum(e, axis=0, keepdims=True))
        d_prob = nt(vals, g)
        delta = jnp.sum(prob * d_prob, axis=0, keepdims=True)
        d_score = prob * (d_prob - delta)
        m = jnp.sum(d_score * raw, axis=0, keepdims=True)
        d2 = (d_score * (s * SCALE)).astype(BF16)
        dk = nn(d2, x)
        dv = nn(prob.astype(BF16), g)
        fac = s * s * s * m * (SCALE / HD)
        hi = fac.astype(BF16).astype(F32)
        lo = fac - hi
        extra = jnp.where(sub16 == 0, hi, jnp.where(sub16 == 1, lo, 0.0)).astype(BF16)
        lhs = jnp.concatenate([d2, extra], axis=0)
        rhs = jnp.concatenate(
            [jnp.concatenate([keys, jnp.zeros((count, HD), BF16)], axis=1), wide16], axis=0
        )
        z = tn(lhs, rhs)
        dx = (z[:, :HD] - x.astype(F32) * z[:, HD:]).astype(BF16)
        for mm in range(MEMBERS):
            c = (h * MEMBERS + mm) * HD
            qg_v[n * BLK : (n + 1) * BLK, c : c + HD] = dx[mm * BLK : (mm + 1) * BLK]
        return dk, dv

    p_load.wait()
    kv_load.wait()

    def pick(slot, h, part):
        c = part * KW + h * HD
        own = p_v[:, c : c + HD].astype(F32)
        got = [cand[k, h, part].astype(F32) for k in range(SPAN - 1)]
        return jnp.where(
            slot == 0, own, jnp.where(slot == 1, got[0], jnp.where(slot == 2, got[1], got[2]))
        )

    def head(h, between):
        q_loads[h].wait()
        g_loads[h].wait()
        k_raw = kv_v[:, h * HD : (h + 1) * HD].astype(F32)
        k_inv = unit_factor(k_raw)
        k_full = k_raw * k_inv * cqk
        k_b = k_full.astype(BF16)
        v_b = kv_v[:, KW + h * HD : KW + (h + 1) * HD]
        p_full, p_b, w_b = [], [], []
        for slot in (slot0, slot1):
            praw = pick(slot, h, 0)
            full = praw * unit_factor(praw) * cqk
            p_full.append(full)
            p_b.append(full.astype(BF16))
            w_b.append(pick(slot, h, 1).astype(BF16))
        dk0, dv0 = attend(
            0, h, jnp.concatenate([k_b[:BLK], p_b[0]], axis=0), jnp.concatenate([v_b[:BLK], w_b[0]], axis=0)
        )
        between()
        dk1, dv1 = attend(1, h, jnp.concatenate([k_b, p_b[1]], axis=0), jnp.concatenate([v_b, w_b[1]], axis=0))
        d_p = [(cq * dk0[BLK:], dv0[BLK:]), (cq * dk1[2 * BLK :], dv1[2 * BLK :])]
        for part in range(2):
            for k in range(SPAN):
                term = jnp.where(slot0 == k, d_p[0][part], 0.0) + jnp.where(slot1 == k, d_p[1][part], 0.0)
                if k == SPAN - 1:
                    gsend[k - 1, h, part] = term.astype(BF16)
                else:
                    parts[k, h, part] = term
        back(SPAN - 2, h).start()
        dk = jnp.concatenate([dk0[:BLK] + dk1[:BLK], dk1[BLK : 2 * BLK]], axis=0)
        dv = jnp.concatenate([dv0[:BLK] + dv1[:BLK], dv1[BLK : 2 * BLK]], axis=0)
        kvg_v[:, h * HD : (h + 1) * HD] = norm_backward(k_raw, k_inv, cqk * dk).astype(BF16)
        kvg_v[:, KW + h * HD : KW + (h + 1) * HD] = dv.astype(BF16)
        return fold8(k_full * dk) + fold8(p_full[0] * dk0[BLK:]) + fold8(p_full[1] * dk1[2 * BLK :])

    def q_out(h):
        cols = pl.ds(h * MEMBERS * HD, MEMBERS * HD)
        return pltpu.make_async_copy(qg_v.at[:, cols], qg_hbm.at[0, :, cols], out_sem.at[h])

    pump(1, 0)
    send(0, 2)
    pump(1, 1)
    pump(2, 0)
    send(0, 3)
    pump(1, 2)
    arrive(2, 0)

    def between0():
        pump(2, 1)

    total = head(0, between0)
    q_out(0).start()
    pump(1, 3)
    pump(2, 2)
    arrive(2, 1)

    def between1():
        pump(2, 3)
        back_step(1, 0)

    total += head(1, between1)
    q_out(1).start()
    arrive(2, 2)
    back_step(0, 0)

    def between2():
        back_step(1, 1)

    total += head(2, between2)
    q_out(2).start()
    arrive(2, 3)
    back_step(0, 1)

    def between3():
        back_step(1, 2)

    total += head(3, between3)
    q_out(3).start()
    kv_out = pltpu.make_async_copy(kvg_v, kvg_hbm.at[0], out_sem.at[KVH])
    kv_out.start()

    def exchange(buf, mine, size, peer_of, send_sem, recv_sem):
        def copy(j):
            return pltpu.make_async_remote_copy(
                src_ref=buf.at[mine],
                dst_ref=buf.at[mine],
                send_sem=send_sem.at[j],
                recv_sem=recv_sem.at[mine],
                device_id=peer_of(j),
                device_id_type=MESH,
            )

        def start_all():
            for j in range(1, size):
                copy(j).start()

        def finish():
            for j in range(1, size):
                other = lax.rem(mine + j, size)
                pltpu.make_async_remote_copy(
                    src_ref=buf.at[other],
                    dst_ref=buf.at[other],
                    send_sem=send_sem.at[j],
                    recv_sem=recv_sem.at[other],
                    device_id=peer_of(j),
                    device_id_type=MESH,
                ).wait_recv()
            return jnp.sum(buf[...], axis=0)

        def drain():
            for j in range(1, size):
                copy(j).wait_send()

        return start_all, finish, drain

    go1, end1, drain1 = exchange(ar1, grp, GS, group_peer, a1_send, a1_recv)
    go2, end2, drain2 = exchange(ar2, my_y, YS, y_peer, a2_send, a2_recv)
    go3, end3, drain3 = exchange(ar3, my_z, ZS, z_peer, a3_send, a3_recv)

    ar1[grp] = total
    go1()
    back_step(0, 2)
    back_step(1, 3)

    def finish_prompt(h):
        back(0, h).wait_recv()
        both = parts[0, h] + grecv[0, h].astype(F32)
        raw = p_v[:, h * HD : (h + 1) * HD].astype(F32)
        pg_v[:, h * HD : (h + 1) * HD] = norm_backward(raw, unit_factor(raw), ck * both[0]).astype(BF16)
        pg_v[:, KW + h * HD : KW + (h + 1) * HD] = both[1].astype(BF16)

    finish_prompt(0)
    finish_prompt(1)
    ar2[my_y] = end1()
    go2()
    back_step(0, 3)
    finish_prompt(2)
    ar3[my_z] = end2()
    go3()
    finish_prompt(3)
    p_out = pltpu.make_async_copy(pg_v, pg_hbm.at[0], out_sem.at[KVH + 1])
    p_out.start()
    summed = jnp.sum(end3(), axis=0, keepdims=True) * (1.0 / math.sqrt(GS * ZS * YS * CT))
    gains_ref[0:1] = summed / cq
    gains_ref[1:2] = summed / ck

    for k in range(SPAN - 1):
        for h in range(KVH):
            for copy in hop(k, h):
                copy.wait_send()
            back(k, h).wait_send()
    drain1()
    drain2()
    drain3()
    for h in range(KVH):
        q_out(h).wait()
    kv_out.wait()
    p_out.wait()


def shards(queries, out_grad, keys_values, prompt_kv, q_gain, k_gain, block_owner, block_start):
    anywhere = pl.BlockSpec(memory_space=pl.ANY)
    vmem = pl.BlockSpec(memory_space=pltpu.VMEM)
    smem = pl.BlockSpec(memory_space=pltpu.SMEM)
    dma = pltpu.SemaphoreType.DMA
    return pl.pallas_call(
        kernel,
        out_shape=(
            jax.ShapeDtypeStruct((1, CT, QW), BF16),
            jax.ShapeDtypeStruct((1, CT, 2 * KW), BF16),
            jax.ShapeDtypeStruct((1, P_SIZE, 2 * KW), BF16),
            jax.ShapeDtypeStruct((2, HD), F32),
        ),
        in_specs=[anywhere] * 4 + [vmem] * 2 + [smem] * 2,
        out_specs=(anywhere, anywhere, anywhere, vmem),
        scratch_shapes=[
            pltpu.VMEM((CT, QW), BF16),
            pltpu.VMEM((CT, QW), BF16),
            pltpu.VMEM((CT, 2 * KW), BF16),
            pltpu.VMEM((P_SIZE, 2 * KW), BF16),
            pltpu.VMEM((CT, QW), BF16),
            pltpu.VMEM((CT, 2 * KW), BF16),
            pltpu.VMEM((P_SIZE, 2 * KW), BF16),
            pltpu.VMEM((SPAN - 1, KVH, 2, P_SIZE, HD), BF16),
            pltpu.VMEM((SPAN - 1, KVH, 2, P_SIZE, HD), F32),
            pltpu.VMEM((SPAN - 1, KVH, 2, P_SIZE, HD), BF16),
            pltpu.VMEM((SPAN - 1, KVH, 2, P_SIZE, HD), BF16),
            pltpu.VMEM((GS, 8, HD), F32),
            pltpu.VMEM((YS, 8, HD), F32),
            pltpu.VMEM((ZS, 8, HD), F32),
            dma((KVH,)),
            dma((KVH,)),
            dma,
            dma,
            dma((KVH + 2,)),
            dma((SPAN - 1, KVH, 2)),
            dma((SPAN - 1, KVH, 2)),
            dma((SPAN - 1, KVH)),
            dma((SPAN - 1, KVH)),
            dma((GS,)),
            dma((GS,)),
            dma((YS,)),
            dma((YS,)),
            dma((ZS,)),
            dma((ZS,)),
        ],
        compiler_params=pltpu.CompilerParams(
            collective_id=0, has_side_effects=True, vmem_limit_bytes=48 * 1024 * 1024
        ),
        name="prefix_attention_grad",
    )(
        queries,
        out_grad,
        keys_values,
        prompt_kv,
        q_gain.reshape(1, HD),
        k_gain.reshape(1, HD),
        block_owner,
        block_start,
    )


def solution(mesh):
    placed = (
        P("group", "dp", None),
        P("group", "dp", None),
        P("group", "dp", None),
        P("group", "dp", None),
        P(),
        P(),
        P("group", "dp"),
        P("group", "dp"),
    )
    return jax.shard_map(
        shards,
        mesh=mesh,
        in_specs=placed,
        out_specs=(P("group", "dp", None), P("group", "dp", None), P("group", "dp", None), P()),
        check_vma=False,
    )
```

```python
import functools
import math

import jax
import jax.numpy as jnp
from jax import lax
from jax.experimental import pallas as pl
from jax.experimental.pallas import tpu as pltpu
from jax.sharding import PartitionSpec as P

H = 32
KVH = 4
HD = 128
BLK = 64
SPAN = 4
P_SIZE = 64
QW = 4096
KW = 512
CT = 128
MEMBERS = H // KVH
ROWS = MEMBERS * BLK
NORM_EPS = 1e-06
SCALE = HD**-0.5
LOG2E = math.log2(math.e)
ZS = 16
YS = 4
GS = 8
F32 = jnp.float32
BF16 = jnp.bfloat16
MESH = pl.DeviceIdType.MESH


def nt(a, b):
    return lax.dot_general(a, b, (((1,), (1,)), ((), ())), preferred_element_type=F32)


def nn(a, b):
    return jnp.dot(a, b, preferred_element_type=F32)


def tn(a, b):
    return lax.dot_general(a, b, (((0,), (0,)), ((), ())), preferred_element_type=F32)


def fold8(a):
    return jnp.sum(a.reshape(a.shape[0] // 8, 8, a.shape[1]), axis=0)


def unit_factor(raw):
    return lax.rsqrt(jnp.mean(raw * raw, axis=-1, keepdims=True) + NORM_EPS)


def norm_backward(raw, inverse, weighted):
    return inverse * weighted - raw * (inverse * inverse * inverse) * jnp.mean(
        raw * weighted, axis=-1, keepdims=True
    )


def kernel(
    q_hbm, g_hbm, kv_hbm, p_hbm, qgain_hbm, kgain_hbm, owner_hbm, start_hbm,
    qg_hbm, kvg_hbm, pg_hbm, gains_ref,
    q_v, g_v, kv_v, p_v, qgain, kgain, owner, start, qg_v, kvg_v, pg_v,
    e_v, d_v, lhs_v, cand, parts, gsend, grecv, ar1, ar2,
    q_sem, g_sem, small_sem, out_sem, f_send, f_recv, b_send, b_recv,
    a1_send, a1_recv, a2_send, a2_recv,
):
    me = lax.axis_index("dp")
    grp = lax.axis_index("group")
    right, left = lax.rem(me + 1, ZS * YS), lax.rem(me + ZS * YS - 1, ZS * YS)
    my_y, my_z = me // ZS, lax.rem(me, ZS)

    def plane_at(j):
        return lax.rem(my_y + j // GS, YS), lax.rem(grp + j % GS, GS)

    def plane_peer(j):
        y, g = plane_at(j)
        return (y * ZS + my_z, g)

    def plane_slot(j):
        y, g = plane_at(j)
        return y * GS + g

    def z_peer(j):
        return (my_y * ZS + lax.rem(my_z + j, ZS), grp)

    def z_slot(j):
        return lax.rem(my_z + j, ZS)

    def ring_steps(j, size):
        return min(j, size - j)

    plane_order = sorted(
        range(1, YS * GS),
        key=lambda j: -ring_steps(j // GS, YS) - ring_steps((j % GS + 1) // 2, GS // 2),
    )
    z_order = sorted(range(1, ZS), key=lambda j: -ring_steps(j, ZS))

    barrier = pltpu.get_barrier_semaphore()
    partners = [(right, grp), (left, grp)]
    partners += [z_peer(j) for j in z_order]
    partners += [plane_peer(j) for j in plane_order]
    for peer in partners:
        pl.semaphore_signal(barrier, inc=1, device_id=peer, device_id_type=MESH)

    small = [
        pltpu.make_async_copy(src, dst, small_sem.at[i])
        for i, (src, dst) in enumerate(
            [
                (kv_hbm.at[0], kv_v),
                (qgain_hbm, qgain),
                (kgain_hbm, kgain),
                (owner_hbm, owner),
                (start_hbm, start),
                (p_hbm.at[0], p_v),
            ]
        )
    ]
    q_loads, g_loads = [], []
    for h in range(KVH):
        cols = pl.ds(h * MEMBERS * HD, MEMBERS * HD)
        q_loads.append(pltpu.make_async_copy(q_hbm.at[0, :, cols], q_v.at[:, cols], q_sem.at[h]))
        g_loads.append(pltpu.make_async_copy(g_hbm.at[0, :, cols], g_v.at[:, cols], g_sem.at[h]))
    for load in small[:3] + [q_loads[0], g_loads[0]] + small[3:] + q_loads[1:] + g_loads[1:]:
        load.start()

    def hop(k, h):
        copies = []
        for part in range(2):
            if k == 0:
                src = p_hbm.at[0, :, pl.ds(part * KW + h * HD, HD)]
            else:
                src = cand.at[k - 1, h, part]
            copies.append(
                pltpu.make_async_remote_copy(
                    src_ref=src,
                    dst_ref=cand.at[k, h, part],
                    send_sem=f_send.at[k, h, part],
                    recv_sem=f_recv.at[k, h, part],
                    device_id=(right, grp),
                    device_id_type=MESH,
                )
            )
        return copies

    def send(k, h):
        for copy in hop(k, h):
            copy.start()

    def arrive(k, h):
        for copy in hop(k, h):
            copy.wait_recv()

    def pump(k, h):
        arrive(k - 1, h)
        send(k, h)

    def back(k, h):
        return pltpu.make_async_remote_copy(
            src_ref=gsend.at[k, h],
            dst_ref=grecv.at[k, h],
            send_sem=b_send.at[k, h],
            recv_sem=b_recv.at[k, h],
            device_id=(left, grp),
            device_id_type=MESH,
        )

    def back_step(k, h):
        back(k + 1, h).wait_recv()
        gsend[k, h] = (parts[k + 1, h] + grecv[k + 1, h].astype(F32)).astype(BF16)
        back(k, h).start()

    def exchange(buf, mine, order, peer_of, slot_of, send_sem, recv_sem):
        def copy(j, slot):
            return pltpu.make_async_remote_copy(
                src_ref=buf.at[slot],
                dst_ref=buf.at[slot],
                send_sem=send_sem.at[j],
                recv_sem=recv_sem.at[slot],
                device_id=peer_of(j),
                device_id_type=MESH,
            )

        def go(value):
            buf[mine] = value
            for j in order:
                copy(j, mine).start()

        def finish():
            for j in reversed(order):
                copy(j, slot_of(j)).wait_recv()
            return jnp.sum(buf[...], axis=0)

        def drain():
            for j in order:
                copy(j, mine).wait_send()

        return go, finish, drain

    go1, end1, drain1 = exchange(
        ar1, my_y * GS + grp, plane_order, plane_peer, plane_slot, a1_send, a1_recv
    )
    go2, end2, drain2 = exchange(ar2, my_z, z_order, z_peer, z_slot, a2_send, a2_recv)

    pl.semaphore_wait(barrier, len(partners))
    for h in range(KVH):
        send(0, h)

    key_at = lax.broadcasted_iota(jnp.int32, (BLK, ROWS), 0)
    row_at = lax.rem(lax.broadcasted_iota(jnp.int32, (BLK, ROWS), 1), BLK)
    tri = key_at <= row_at
    ones8 = jnp.ones((8, HD), BF16)
    sub16 = lax.broadcasted_iota(jnp.int32, (16, ROWS), 0)
    wide16 = jnp.concatenate(
        [
            jnp.zeros((16, HD), BF16),
            jnp.where(lax.broadcasted_iota(jnp.int32, (16, HD), 0) < 2, 1.0, 0.0).astype(BF16),
        ],
        axis=1,
    )
    for load in small:
        load.wait()
    cq = qgain[...]
    ck = kgain[...]
    cqk = cq * ck
    slots = (me - owner[0, 0], me - owner[0, 1])
    same = jnp.where((start[0, 1] == 1) | (owner[0, 0] != owner[0, 1]), 0.0, 1.0).astype(F32)

    def rows_of(ref, n, h):
        return jnp.concatenate(
            [
                ref[n * BLK : (n + 1) * BLK, (h * MEMBERS + m) * HD : (h * MEMBERS + m + 1) * HD]
                for m in range(MEMBERS)
            ],
            axis=0,
        )

    def local_keys(h):
        raw = kv_v[:, h * HD : (h + 1) * HD].astype(F32)
        inverse = unit_factor(raw)
        return raw, inverse, raw * inverse * cqk

    def over_keys(a):
        return jnp.sum(a, axis=0, keepdims=True)

    stats = {}

    def before(h):
        q_loads[h].wait()
        g_loads[h].wait()
        k_b = local_keys(h)[2].astype(BF16)
        v_b = kv_v[:, KW + h * HD : KW + (h + 1) * HD]
        for n in range(2):
            count = (n + 1) * BLK
            at = n * BLK
            x = rows_of(q_v, n, h)
            g = rows_of(g_v, n, h)
            s = lax.rsqrt(nt(ones8, x * x)[0:1] * (1.0 / HD) + NORM_EPS)
            raw = nt(k_b[:count], x)
            e = jnp.exp2(raw * (s * (SCALE * LOG2E)))
            if n == 0:
                e = jnp.where(tri, e, 0.0)
            else:
                e = jnp.concatenate([e[:BLK] * same, jnp.where(tri, e[BLK:], 0.0)], axis=0)
            d = nt(v_b[:count], g)
            e_v[h, at : at + count] = e
            d_v[h, at : at + count] = d
            er = e * raw
            stats[h, n] = (s, over_keys(e), over_keys(e * d), over_keys(er), over_keys(er * d))

    def pick(slot, h, part):
        c = part * KW + h * HD
        own = p_v[:, c : c + HD].astype(F32)
        got = [cand[k, h, part].astype(F32) for k in range(SPAN - 1)]
        return jnp.where(
            slot == 0, own, jnp.where(slot == 1, got[0], jnp.where(slot == 2, got[1], got[2]))
        )

    kept = {}

    def middle(h):
        arrive(SPAN - 2, h)
        full_l = local_keys(h)[2]
        k_b = full_l.astype(BF16)
        d_p, dks, dvs = [], [], []
        total = jnp.zeros((8, HD), F32)
        for n in range(2):
            count = (n + 1) * BLK
            at = n * BLK
            praw = pick(slots[n], h, 0)
            full = praw * unit_factor(praw) * cqk
            p_b = full.astype(BF16)
            w_b = pick(slots[n], h, 1).astype(BF16)
            x = rows_of(q_v, n, h)
            g = rows_of(g_v, n, h)
            s, t, u, xs, ws = stats[h, n]
            raw = nt(p_b, x)
            e_p = jnp.exp2(raw * (s * (SCALE * LOG2E)))
            d_prob = nt(w_b, g)
            inv = 1.0 / (t + over_keys(e_p))
            e_d = e_p * d_prob
            er = e_p * raw
            delta = (u + over_keys(e_d)) * inv
            m = (ws + over_keys(er * d_prob) - delta * (xs + over_keys(er))) * inv
            r = s * SCALE
            prob_l = e_v[h, at : at + count] * inv
            prob_p = e_p * inv
            d2 = jnp.concatenate(
                [
                    (prob_l * ((d_v[h, at : at + count] - delta) * r)).astype(BF16),
                    (prob_p * ((d_prob - delta) * r)).astype(BF16),
                ],
                axis=0,
            )
            prob = jnp.concatenate([prob_l.astype(BF16), prob_p.astype(BF16)], axis=0)
            dk = nn(d2, x)
            dv = nn(prob, g)
            fac = s * s * s * m * (SCALE / HD)
            hi = fac.astype(BF16).astype(F32)
            extra = jnp.where(sub16 == 0, hi, jnp.where(sub16 == 1, fac - hi, 0.0)).astype(BF16)
            lhs_v[h, n, : count + BLK] = d2
            lhs_v[h, n, count + BLK : count + BLK + 16] = extra
            kept[h, n] = jnp.concatenate([k_b[:count], p_b], axis=0)
            d_p.append((cq * dk[count:], dv[count:]))
            dks.append(dk[:count])
            dvs.append(dv[:count])
            total += fold8(full * dk[count:])
        for part in range(2):
            for k in range(SPAN):
                term = jnp.where(slots[0] == k, d_p[0][part], 0.0) + jnp.where(
                    slots[1] == k, d_p[1][part], 0.0
                )
                if k == SPAN - 1:
                    gsend[k - 1, h, part] = term.astype(BF16)
                else:
                    parts[k, h, part] = term
        back(SPAN - 2, h).start()
        dk = jnp.concatenate([dks[0] + dks[1][:BLK], dks[1][BLK:]], axis=0)
        dv = jnp.concatenate([dvs[0] + dvs[1][:BLK], dvs[1][BLK:]], axis=0)
        kvg_v[:, KW + h * HD : KW + (h + 1) * HD] = dv.astype(BF16)
        kept[h] = dk
        return total + fold8(full_l * dk)

    def q_out(h):
        cols = pl.ds(h * MEMBERS * HD, MEMBERS * HD)
        return pltpu.make_async_copy(qg_v.at[:, cols], qg_hbm.at[0, :, cols], out_sem.at[h])

    def after(h):
        raw_l, inverse, _ = local_keys(h)
        kvg_v[:, h * HD : (h + 1) * HD] = norm_backward(raw_l, inverse, cqk * kept[h]).astype(BF16)
        for n in range(2):
            count = (n + 2) * BLK
            rhs = jnp.concatenate(
                [jnp.concatenate([kept[h, n], jnp.zeros((count, HD), BF16)], axis=1), wide16], axis=0
            )
            z = tn(lhs_v[h, n, : count + 16], rhs)
            x = rows_of(q_v, n, h).astype(F32)
            dx = (z[:, :HD] - x * z[:, HD:]).astype(BF16)
            for m in range(MEMBERS):
                c = (h * MEMBERS + m) * HD
                qg_v[n * BLK : (n + 1) * BLK, c : c + HD] = dx[m * BLK : (m + 1) * BLK]
        q_out(h).start()

    for h in range(KVH - 1):
        before(h)
    for h in range(KVH):
        pump(1, h)
    before(KVH - 1)
    for h in range(KVH):
        pump(2, h)
    total = middle(0)
    for h in range(1, KVH):
        total += middle(h)
    go1(jnp.sum(total, axis=0, keepdims=True))

    back_step(1, 0)
    back_step(1, 1)
    after(0)
    back_step(1, 2)
    back_step(1, 3)
    go2(end1())
    back_step(0, 0)
    after(1)
    back_step(0, 1)
    after(2)
    back_step(0, 2)
    after(3)
    kv_out = pltpu.make_async_copy(kvg_v, kvg_hbm.at[0], out_sem.at[KVH])
    kv_out.start()
    back_step(0, 3)

    def finish_prompt(h):
        back(0, h).wait_recv()
        both = parts[0, h] + grecv[0, h].astype(F32)
        raw = p_v[:, h * HD : (h + 1) * HD].astype(F32)
        pg_v[:, h * HD : (h + 1) * HD] = norm_backward(raw, unit_factor(raw), ck * both[0]).astype(BF16)
        pg_v[:, KW + h * HD : KW + (h + 1) * HD] = both[1].astype(BF16)

    for h in range(KVH):
        finish_prompt(h)
    p_out = pltpu.make_async_copy(pg_v, pg_hbm.at[0], out_sem.at[KVH + 1])
    p_out.start()
    for k in range(SPAN - 1):
        for h in range(KVH):
            for copy in hop(k, h):
                copy.wait_send()
            back(k, h).wait_send()
    drain1()
    for h in range(KVH):
        q_out(h).wait()
    kv_out.wait()
    summed = end2() * (1.0 / math.sqrt(GS * ZS * YS * CT))
    gains_ref[0:1] = summed / cq
    gains_ref[1:2] = summed / ck
    drain2()
    p_out.wait()


def shards(queries, out_grad, keys_values, prompt_kv, q_gain, k_gain, block_owner, block_start):
    hbm = pl.BlockSpec(memory_space=pltpu.HBM)
    anywhere = pl.BlockSpec(memory_space=pl.ANY)
    vmem = pl.BlockSpec(memory_space=pltpu.VMEM)
    dma = pltpu.SemaphoreType.DMA
    return pl.pallas_call(
        kernel,
        out_shape=(
            jax.ShapeDtypeStruct((1, CT, QW), BF16),
            jax.ShapeDtypeStruct((1, CT, 2 * KW), BF16),
            jax.ShapeDtypeStruct((1, P_SIZE, 2 * KW), BF16),
            jax.ShapeDtypeStruct((2, HD), F32),
        ),
        in_specs=[hbm] * 8,
        out_specs=(anywhere, anywhere, anywhere, vmem),
        scratch_shapes=[
            pltpu.VMEM((CT, QW), BF16),
            pltpu.VMEM((CT, QW), BF16),
            pltpu.VMEM((CT, 2 * KW), BF16),
            pltpu.VMEM((P_SIZE, 2 * KW), BF16),
            pltpu.VMEM((1, HD), F32),
            pltpu.VMEM((1, HD), F32),
            pltpu.SMEM((1, 2), jnp.int32),
            pltpu.SMEM((1, 2), jnp.int32),
            pltpu.VMEM((CT, QW), BF16),
            pltpu.VMEM((CT, 2 * KW), BF16),
            pltpu.VMEM((P_SIZE, 2 * KW), BF16),
            pltpu.VMEM((KVH, 3 * BLK, ROWS), F32),
            pltpu.VMEM((KVH, 3 * BLK, ROWS), F32),
            pltpu.VMEM((KVH, 2, 3 * BLK + 16, ROWS), BF16),
            pltpu.VMEM((SPAN - 1, KVH, 2, P_SIZE, HD), BF16),
            pltpu.VMEM((SPAN - 1, KVH, 2, P_SIZE, HD), F32),
            pltpu.VMEM((SPAN - 1, KVH, 2, P_SIZE, HD), BF16),
            pltpu.VMEM((SPAN - 1, KVH, 2, P_SIZE, HD), BF16),
            pltpu.VMEM((YS * GS, 1, HD), F32),
            pltpu.VMEM((ZS, 1, HD), F32),
            dma((KVH,)),
            dma((KVH,)),
            dma((6,)),
            dma((KVH + 2,)),
            dma((SPAN - 1, KVH, 2)),
            dma((SPAN - 1, KVH, 2)),
            dma((SPAN - 1, KVH)),
            dma((SPAN - 1, KVH)),
            dma((YS * GS,)),
            dma((YS * GS,)),
            dma((ZS,)),
            dma((ZS,)),
        ],
        compiler_params=pltpu.CompilerParams(
            collective_id=0, has_side_effects=True, vmem_limit_bytes=60 * 1024 * 1024
        ),
        name="prefix_attention_grad",
    )(
        queries,
        out_grad,
        keys_values,
        prompt_kv,
        q_gain.reshape(1, HD),
        k_gain.reshape(1, HD),
        block_owner,
        block_start,
    )


def solution(mesh):
    placed = (
        P("group", "dp", None),
        P("group", "dp", None),
        P("group", "dp", None),
        P("group", "dp", None),
        P(),
        P(),
        P("group", "dp"),
        P("group", "dp"),
    )
    return jax.shard_map(
        shards,
        mesh=mesh,
        in_specs=placed,
        out_specs=(P("group", "dp", None), P("group", "dp", None), P("group", "dp", None), P()),
        check_vma=False,
    )
```

```python
import functools
import math

import jax
import jax.numpy as jnp
from jax import lax
from jax.experimental import pallas as pl
from jax.experimental.pallas import tpu as pltpu
from jax.sharding import PartitionSpec as P

H = 32
KVH = 4
HD = 128
BLK = 64
SPAN = 4
P_SIZE = 64
QW = 4096
KW = 512
CT = 128
MEMBERS = H // KVH
ROWS = MEMBERS * BLK
NORM_EPS = 1e-06
SCALE = HD**-0.5
LOG2E = math.log2(math.e)
ZS = 16
YS = 4
GS = 8
F32 = jnp.float32
BF16 = jnp.bfloat16
MESH = pl.DeviceIdType.MESH


def nt(a, b):
    return lax.dot_general(a, b, (((1,), (1,)), ((), ())), preferred_element_type=F32)


def nn(a, b):
    return jnp.dot(a, b, preferred_element_type=F32)


def tn(a, b):
    return lax.dot_general(a, b, (((0,), (0,)), ((), ())), preferred_element_type=F32)


def fold8(a):
    return jnp.sum(a.reshape(a.shape[0] // 8, 8, a.shape[1]), axis=0)


def unit_factor(raw):
    return lax.rsqrt(jnp.mean(raw * raw, axis=-1, keepdims=True) + NORM_EPS)


def norm_backward(raw, inverse, weighted):
    return inverse * weighted - raw * (inverse * inverse * inverse) * jnp.mean(
        raw * weighted, axis=-1, keepdims=True
    )


def kernel(
    q_hbm, g_hbm, kv_hbm, p_hbm, qgain_hbm, kgain_hbm, owner_hbm, start_hbm,
    qg_v, kvg_v, pg_v, gains_ref,
    q_v, g_v, kv_v, own, qgain, kgain, owner, start,
    e_v, d_v, lhs_v, cand, parts, gsend, grecv, ar1, ar2,
    q_sem, g_sem, small_sem, own_sem, f_send, f_recv, b_send, b_recv,
    a1_send, a1_recv, a2_send, a2_recv, known,
):
    me = lax.axis_index("dp")
    grp = lax.axis_index("group")
    right, left = lax.rem(me + 1, ZS * YS), lax.rem(me + ZS * YS - 1, ZS * YS)
    my_y, my_z = me // ZS, lax.rem(me, ZS)

    def plane_at(j):
        return lax.rem(my_y + j // GS, YS), lax.rem(grp + j % GS, GS)

    def plane_peer(j):
        y, g = plane_at(j)
        return (y * ZS + my_z, g)

    def plane_slot(j):
        y, g = plane_at(j)
        return y * GS + g

    def z_peer(j):
        return (my_y * ZS + lax.rem(my_z + j, ZS), grp)

    def z_slot(j):
        return lax.rem(my_z + j, ZS)

    def ring_steps(j, size):
        return min(j, size - j)

    plane_order = sorted(
        range(1, YS * GS),
        key=lambda j: -ring_steps(j // GS, YS) - ring_steps((j % GS + 1) // 2, GS // 2),
    )
    z_order = sorted(range(1, ZS), key=lambda j: -ring_steps(j, ZS))

    def x_peer(j):
        return (me, lax.rem(grp + 2 * j, GS))

    def y_peer(j):
        return (lax.rem(my_y + j, YS) * ZS + my_z, grp)

    other_core = (me, grp + 1 - 2 * lax.rem(grp, 2))
    beside = [y_peer(1), y_peer(YS - 1), x_peer(1), x_peer(GS // 2 - 1), other_core]
    rounds = [
        beside + [z_peer(1), z_peer(ZS - 1)],
        beside + [y_peer(2), x_peer(2), z_peer(2), z_peer(ZS - 2)],
        [other_core, z_peer(4), z_peer(ZS - 4)],
    ]

    def tell(i):
        for peer in rounds[i]:
            pl.semaphore_signal(known.at[i], inc=1, device_id=peer, device_id_type=MESH)

    def hear(i):
        pl.semaphore_wait(known.at[i], len(rounds[i]))

    barrier = pltpu.get_barrier_semaphore()
    partners = [(right, grp), (left, grp)] + rounds[0]
    for peer in partners:
        pl.semaphore_signal(barrier, inc=1, device_id=peer, device_id_type=MESH)

    small = [
        pltpu.make_async_copy(src, dst, small_sem.at[i])
        for i, (src, dst) in enumerate(
            [
                (kv_hbm.at[0], kv_v),
                (qgain_hbm, qgain),
                (kgain_hbm, kgain),
                (owner_hbm, owner),
                (start_hbm, start),
            ]
        )
    ]
    own_loads = [
        pltpu.make_async_copy(
            p_hbm.at[0, :, pl.ds(part * KW + h * HD, HD)], own.at[h, part], own_sem.at[h, part]
        )
        for h in range(KVH)
        for part in range(2)
    ]
    q_loads, g_loads = [], []
    for h in range(KVH):
        cols = pl.ds(h * MEMBERS * HD, MEMBERS * HD)
        q_loads.append(pltpu.make_async_copy(q_hbm.at[0, :, cols], q_v.at[:, cols], q_sem.at[h]))
        g_loads.append(pltpu.make_async_copy(g_hbm.at[0, :, cols], g_v.at[:, cols], g_sem.at[h]))
    for load in own_loads + small + [q_loads[0], g_loads[0]] + q_loads[1:] + g_loads[1:]:
        load.start()

    def hop(k, h):
        return pltpu.make_async_remote_copy(
            src_ref=own.at[h] if k == 0 else cand.at[k - 1, h],
            dst_ref=cand.at[k, h],
            send_sem=f_send.at[k, h],
            recv_sem=f_recv.at[k, h],
            device_id=(right, grp),
            device_id_type=MESH,
        )

    def pump(k, h):
        hop(k - 1, h).wait_recv()
        hop(k, h).start()

    def back(k, h):
        return pltpu.make_async_remote_copy(
            src_ref=gsend.at[k, h],
            dst_ref=grecv.at[k, h],
            send_sem=b_send.at[k, h],
            recv_sem=b_recv.at[k, h],
            device_id=(left, grp),
            device_id_type=MESH,
        )

    def back_step(k, h):
        back(k + 1, h).wait_recv()
        gsend[k, h] = (parts[k + 1, h] + grecv[k + 1, h].astype(F32)).astype(BF16)
        back(k, h).start()

    def exchange(buf, mine, order, peer_of, slot_of, send_sem, recv_sem):
        def copy(j, slot):
            return pltpu.make_async_remote_copy(
                src_ref=buf.at[slot],
                dst_ref=buf.at[slot],
                send_sem=send_sem.at[j],
                recv_sem=recv_sem.at[slot],
                device_id=peer_of(j),
                device_id_type=MESH,
            )

        def go(value):
            buf[mine] = value
            for j in order:
                copy(j, mine).start()

        def finish():
            for j in reversed(order):
                copy(j, slot_of(j)).wait_recv()
            return jnp.sum(buf[...], axis=0)

        def drain():
            for j in order:
                copy(j, mine).wait_send()

        return go, finish, drain

    go1, end1, drain1 = exchange(
        ar1, my_y * GS + grp, plane_order, plane_peer, plane_slot, a1_send, a1_recv
    )
    go2, end2, drain2 = exchange(ar2, my_z, z_order, z_peer, z_slot, a2_send, a2_recv)

    for load in own_loads:
        load.wait()
    pl.semaphore_wait(barrier, len(partners))
    for h in range(KVH):
        hop(0, h).start()
    tell(0)

    key_at = lax.broadcasted_iota(jnp.int32, (BLK, ROWS), 0)
    row_at = lax.rem(lax.broadcasted_iota(jnp.int32, (BLK, ROWS), 1), BLK)
    tri = key_at <= row_at
    ones8 = jnp.ones((8, HD), BF16)
    sub16 = lax.broadcasted_iota(jnp.int32, (16, ROWS), 0)
    wide16 = jnp.concatenate(
        [
            jnp.zeros((16, HD), BF16),
            jnp.where(lax.broadcasted_iota(jnp.int32, (16, HD), 0) < 2, 1.0, 0.0).astype(BF16),
        ],
        axis=1,
    )
    for load in small:
        load.wait()
    cq = qgain[...]
    ck = kgain[...]
    cqk = cq * ck
    slots = (me - owner[0, 0], me - owner[0, 1])
    same = jnp.where((start[0, 1] == 1) | (owner[0, 0] != owner[0, 1]), 0.0, 1.0).astype(F32)

    def rows_of(ref, n, h):
        return jnp.concatenate(
            [
                ref[n * BLK : (n + 1) * BLK, (h * MEMBERS + m) * HD : (h * MEMBERS + m + 1) * HD]
                for m in range(MEMBERS)
            ],
            axis=0,
        )

    def local_keys(h):
        raw = kv_v[:, h * HD : (h + 1) * HD].astype(F32)
        inverse = unit_factor(raw)
        return raw, inverse, raw * inverse * cqk

    def over_keys(a):
        return jnp.sum(a, axis=0, keepdims=True)

    stats = {}

    def before(h):
        q_loads[h].wait()
        g_loads[h].wait()
        k_b = local_keys(h)[2].astype(BF16)
        v_b = kv_v[:, KW + h * HD : KW + (h + 1) * HD]
        for n in range(2):
            count = (n + 1) * BLK
            at = n * BLK
            x = rows_of(q_v, n, h)
            g = rows_of(g_v, n, h)
            s = lax.rsqrt(nt(ones8, x * x)[0:1] * (1.0 / HD) + NORM_EPS)
            raw = nt(k_b[:count], x)
            e = jnp.exp2(raw * (s * (SCALE * LOG2E)))
            if n == 0:
                e = jnp.where(tri, e, 0.0)
            else:
                e = jnp.concatenate([e[:BLK] * same, jnp.where(tri, e[BLK:], 0.0)], axis=0)
            d = nt(v_b[:count], g)
            e_v[h, at : at + count] = e
            d_v[h, at : at + count] = d
            er = e * raw
            stats[h, n] = (s, over_keys(e), over_keys(e * d), over_keys(er), over_keys(er * d))

    def pick(slot, h, part):
        mine = own[h, part].astype(F32)
        got = [cand[k, h, part].astype(F32) for k in range(SPAN - 1)]
        return jnp.where(
            slot == 0, mine, jnp.where(slot == 1, got[0], jnp.where(slot == 2, got[1], got[2]))
        )

    kept = {}

    def middle(h):
        hop(SPAN - 2, h).wait_recv()
        full_l = local_keys(h)[2]
        k_b = full_l.astype(BF16)
        d_p, dks, dvs = [], [], []
        total = jnp.zeros((8, HD), F32)
        for n in range(2):
            count = (n + 1) * BLK
            at = n * BLK
            praw = pick(slots[n], h, 0)
            full = praw * unit_factor(praw) * cqk
            p_b = full.astype(BF16)
            w_b = pick(slots[n], h, 1).astype(BF16)
            x = rows_of(q_v, n, h)
            g = rows_of(g_v, n, h)
            s, t, u, xs, ws = stats[h, n]
            raw = nt(p_b, x)
            e_p = jnp.exp2(raw * (s * (SCALE * LOG2E)))
            d_prob = nt(w_b, g)
            inv = 1.0 / (t + over_keys(e_p))
            e_d = e_p * d_prob
            er = e_p * raw
            delta = (u + over_keys(e_d)) * inv
            m = (ws + over_keys(er * d_prob) - delta * (xs + over_keys(er))) * inv
            r = s * SCALE
            prob_l = e_v[h, at : at + count] * inv
            prob_p = e_p * inv
            d2 = jnp.concatenate(
                [
                    (prob_l * ((d_v[h, at : at + count] - delta) * r)).astype(BF16),
                    (prob_p * ((d_prob - delta) * r)).astype(BF16),
                ],
                axis=0,
            )
            prob = jnp.concatenate([prob_l.astype(BF16), prob_p.astype(BF16)], axis=0)
            dk = nn(d2, x)
            dv = nn(prob, g)
            fac = s * s * s * m * (SCALE / HD)
            hi = fac.astype(BF16).astype(F32)
            extra = jnp.where(sub16 == 0, hi, jnp.where(sub16 == 1, fac - hi, 0.0)).astype(BF16)
            lhs_v[h, n, : count + BLK] = d2
            lhs_v[h, n, count + BLK : count + BLK + 16] = extra
            kept[h, n] = jnp.concatenate([k_b[:count], p_b], axis=0)
            d_p.append((cq * dk[count:], dv[count:]))
            dks.append(dk[:count])
            dvs.append(dv[:count])
            total += fold8(full * dk[count:])
        for part in range(2):
            for k in range(SPAN):
                term = jnp.where(slots[0] == k, d_p[0][part], 0.0) + jnp.where(
                    slots[1] == k, d_p[1][part], 0.0
                )
                if k == SPAN - 1:
                    gsend[k - 1, h, part] = term.astype(BF16)
                else:
                    parts[k, h, part] = term
        back(SPAN - 2, h).start()
        dk = jnp.concatenate([dks[0] + dks[1][:BLK], dks[1][BLK:]], axis=0)
        dv = jnp.concatenate([dvs[0] + dvs[1][:BLK], dvs[1][BLK:]], axis=0)
        kvg_v[0, :, KW + h * HD : KW + (h + 1) * HD] = dv.astype(BF16)
        kept[h] = dk
        return total + fold8(full_l * dk)

    def after(h):
        raw_l, inverse, _ = local_keys(h)
        kvg_v[0, :, h * HD : (h + 1) * HD] = norm_backward(raw_l, inverse, cqk * kept[h]).astype(BF16)
        for n in range(2):
            count = (n + 2) * BLK
            rhs = jnp.concatenate(
                [jnp.concatenate([kept[h, n], jnp.zeros((count, HD), BF16)], axis=1), wide16], axis=0
            )
            z = tn(lhs_v[h, n, : count + 16], rhs)
            x = rows_of(q_v, n, h).astype(F32)
            dx = (z[:, :HD] - x * z[:, HD:]).astype(BF16)
            for m in range(MEMBERS):
                c = (h * MEMBERS + m) * HD
                qg_v[0, n * BLK : (n + 1) * BLK, c : c + HD] = dx[m * BLK : (m + 1) * BLK]

    before(0)
    hear(0)
    tell(1)
    before(1)
    before(2)
    for h in range(KVH):
        pump(1, h)
    hear(1)
    tell(2)
    before(3)
    for h in range(KVH):
        pump(2, h)
    total = middle(0)
    for h in range(1, KVH):
        total += middle(h)
    hear(2)
    go1(jnp.sum(total, axis=0, keepdims=True))

    back_step(1, 0)
    back_step(1, 1)
    after(0)
    back_step(1, 2)
    back_step(1, 3)
    go2(end1())
    back_step(0, 0)
    after(1)
    back_step(0, 1)
    after(2)
    back_step(0, 2)
    after(3)
    back_step(0, 3)

    def finish_prompt(h):
        back(0, h).wait_recv()
        both = parts[0, h] + grecv[0, h].astype(F32)
        raw = own[h, 0].astype(F32)
        pg_v[0, :, h * HD : (h + 1) * HD] = norm_backward(raw, unit_factor(raw), ck * both[0]).astype(BF16)
        pg_v[0, :, KW + h * HD : KW + (h + 1) * HD] = both[1].astype(BF16)

    for h in range(KVH):
        finish_prompt(h)
    for k in range(SPAN - 1):
        for h in range(KVH):
            hop(k, h).wait_send()
            back(k, h).wait_send()
    drain1()
    summed = end2() * (1.0 / math.sqrt(GS * ZS * YS * CT))
    gains_ref[0:1] = summed / cq
    gains_ref[1:2] = summed / ck
    drain2()


def shards(queries, out_grad, keys_values, prompt_kv, q_gain, k_gain, block_owner, block_start):
    hbm = pl.BlockSpec(memory_space=pltpu.HBM)
    anywhere = pl.BlockSpec(memory_space=pl.ANY)
    vmem = pl.BlockSpec(memory_space=pltpu.VMEM)
    dma = pltpu.SemaphoreType.DMA
    held = pl.pallas_call(
        kernel,
        out_shape=(
            pltpu.VMEM((1, CT, QW), BF16),
            pltpu.VMEM((1, CT, 2 * KW), BF16),
            pltpu.VMEM((1, P_SIZE, 2 * KW), BF16),
            pltpu.VMEM((2, HD), F32),
        ),
        in_specs=[hbm] * 8,
        out_specs=(vmem, vmem, vmem, vmem),
        scratch_shapes=[
            pltpu.VMEM((CT, QW), BF16),
            pltpu.VMEM((CT, QW), BF16),
            pltpu.VMEM((CT, 2 * KW), BF16),
            pltpu.VMEM((KVH, 2, P_SIZE, HD), BF16),
            pltpu.VMEM((1, HD), F32),
            pltpu.VMEM((1, HD), F32),
            pltpu.SMEM((1, 2), jnp.int32),
            pltpu.SMEM((1, 2), jnp.int32),
            pltpu.VMEM((KVH, 3 * BLK, ROWS), F32),
            pltpu.VMEM((KVH, 3 * BLK, ROWS), F32),
            pltpu.VMEM((KVH, 2, 3 * BLK + 16, ROWS), BF16),
            pltpu.VMEM((SPAN - 1, KVH, 2, P_SIZE, HD), BF16),
            pltpu.VMEM((SPAN - 1, KVH, 2, P_SIZE, HD), F32),
            pltpu.VMEM((SPAN - 1, KVH, 2, P_SIZE, HD), BF16),
            pltpu.VMEM((SPAN - 1, KVH, 2, P_SIZE, HD), BF16),
            pltpu.VMEM((YS * GS, 1, HD), F32),
            pltpu.VMEM((ZS, 1, HD), F32),
            dma((KVH,)),
            dma((KVH,)),
            dma((5,)),
            dma((KVH, 2)),
            dma((SPAN - 1, KVH)),
            dma((SPAN - 1, KVH)),
            dma((SPAN - 1, KVH)),
            dma((SPAN - 1, KVH)),
            dma((YS * GS,)),
            dma((YS * GS,)),
            dma((ZS,)),
            dma((ZS,)),
            pltpu.SemaphoreType.REGULAR((3,)),
        ],
        compiler_params=pltpu.CompilerParams(
            collective_id=0, has_side_effects=True, vmem_limit_bytes=60 * 1024 * 1024
        ),
        name="prefix_attention_grad",
    )(
        queries,
        out_grad,
        keys_values,
        prompt_kv,
        q_gain.reshape(1, HD),
        k_gain.reshape(1, HD),
        block_owner,
        block_start,
    )
    return pl.pallas_call(
        hand_over,
        out_shape=tuple(jax.ShapeDtypeStruct(a.shape, a.dtype) for a in held),
        in_specs=[vmem] * 4,
        out_specs=(anywhere,) * 4,
        scratch_shapes=[dma((KVH * 2 + 3,))],
        compiler_params=pltpu.CompilerParams(vmem_limit_bytes=8 * 1024 * 1024),
        name="hand_over",
    )(*held)


def hand_over(qg, kvg, pg, gains, qg_out, kvg_out, pg_out, gains_out, sem):
    copies = []
    for i in range(2 * KVH):
        rows = pl.ds(i * 16, 16)
        copies.append(pltpu.make_async_copy(qg.at[0, rows], qg_out.at[0, rows], sem.at[i]))
    copies.append(pltpu.make_async_copy(kvg, kvg_out, sem.at[2 * KVH]))
    copies.append(pltpu.make_async_copy(pg, pg_out, sem.at[2 * KVH + 1]))
    copies.append(pltpu.make_async_copy(gains, gains_out, sem.at[2 * KVH + 2]))
    for copy in copies:
        copy.start()
    for copy in copies:
        copy.wait()


def solution(mesh):
    placed = (
        P("group", "dp", None),
        P("group", "dp", None),
        P("group", "dp", None),
        P("group", "dp", None),
        P(),
        P(),
        P("group", "dp"),
        P("group", "dp"),
    )
    return jax.shard_map(
        shards,
        mesh=mesh,
        in_specs=placed,
        out_specs=(P("group", "dp", None), P("group", "dp", None), P("group", "dp", None), P()),
        check_vma=False,
    )
```

```python
import functools
import math

import jax
import jax.numpy as jnp
from jax import lax
from jax.experimental import pallas as pl
from jax.experimental.pallas import tpu as pltpu
from jax.sharding import PartitionSpec as P

H = 32
KVH = 4
HD = 128
BLK = 64
SPAN = 4
P_SIZE = 64
QW = 4096
KW = 512
CT = 128
MEMBERS = H // KVH
ROWS = MEMBERS * BLK
NORM_EPS = 1e-06
SCALE = HD**-0.5
LOG2E = math.log2(math.e)
LATE = 2
ZS = 16
YS = 4
GS = 8
F32 = jnp.float32
BF16 = jnp.bfloat16
MESH = pl.DeviceIdType.MESH


def nt(a, b):
    return lax.dot_general(a, b, (((1,), (1,)), ((), ())), preferred_element_type=F32)


def nn(a, b):
    return jnp.dot(a, b, preferred_element_type=F32)


def tn(a, b):
    return lax.dot_general(a, b, (((0,), (0,)), ((), ())), preferred_element_type=F32)


def fold8(a):
    return jnp.sum(a.reshape(a.shape[0] // 8, 8, a.shape[1]), axis=0)


def unit_factor(raw):
    return lax.rsqrt(jnp.mean(raw * raw, axis=-1, keepdims=True) + NORM_EPS)


def norm_backward(raw, inverse, weighted):
    return inverse * weighted - raw * (inverse * inverse * inverse) * jnp.mean(
        raw * weighted, axis=-1, keepdims=True
    )


def kernel(
    q_hbm, g_hbm, kv_hbm, p_hbm, qgain_hbm, kgain_hbm, owner_hbm, start_hbm,
    qg_v, kvg_v, pg_v, gains_ref,
    q_v, g_v, kv_v, own, qgain, kgain, owner, start,
    e_v, d_v, lhs_v, cand, parts, gsend, grecv, prob_v, ar1, ar2,
    q_sem, g_sem, small_sem, own_sem, f_send, f_recv, b_send, b_recv,
    a1_send, a1_recv, a2_send, a2_recv, known,
):
    me = lax.axis_index("dp")
    grp = lax.axis_index("group")
    right, left = lax.rem(me + 1, ZS * YS), lax.rem(me + ZS * YS - 1, ZS * YS)
    my_y, my_z = me // ZS, lax.rem(me, ZS)

    def plane_at(j):
        return lax.rem(my_y + j // GS, YS), lax.rem(grp + j % GS, GS)

    def plane_peer(j):
        y, g = plane_at(j)
        return (y * ZS + my_z, g)

    def z_peer(j):
        return (my_y * ZS + lax.rem(my_z + j, ZS), grp)

    def ring_steps(j, size):
        return min(j, size - j)

    plane_order = sorted(
        range(1, YS * GS),
        key=lambda j: -ring_steps(j // GS, YS) - ring_steps((j % GS + 1) // 2, GS // 2),
    )
    z_order = sorted(range(1, ZS), key=lambda j: -ring_steps(j, ZS))

    def x_peer(j):
        return (me, lax.rem(grp + 2 * j, GS))

    def y_peer(j):
        return (lax.rem(my_y + j, YS) * ZS + my_z, grp)

    other_core = (me, grp + 1 - 2 * lax.rem(grp, 2))
    beside = [y_peer(1), y_peer(YS - 1), x_peer(1), x_peer(GS // 2 - 1), other_core]
    rounds = [
        beside + [z_peer(1), z_peer(ZS - 1)],
        beside + [y_peer(2), x_peer(2), z_peer(2), z_peer(ZS - 2)],
        [other_core, z_peer(4), z_peer(ZS - 4)],
    ]

    def tell(i):
        for peer in rounds[i]:
            pl.semaphore_signal(known.at[i], inc=1, device_id=peer, device_id_type=MESH)

    def hear(i):
        pl.semaphore_wait(known.at[i], len(rounds[i]))

    barrier = pltpu.get_barrier_semaphore()
    partners = [(right, grp), (left, grp)] + rounds[0]
    for peer in partners:
        pl.semaphore_signal(barrier, inc=1, device_id=peer, device_id_type=MESH)

    small = [
        pltpu.make_async_copy(src, dst, small_sem.at[i])
        for i, (src, dst) in enumerate(
            [
                (kv_hbm.at[0], kv_v),
                (qgain_hbm, qgain),
                (kgain_hbm, kgain),
                (owner_hbm, owner),
                (start_hbm, start),
            ]
        )
    ]
    own_loads = [
        pltpu.make_async_copy(
            p_hbm.at[0, :, pl.ds(part * KW + h * HD, HD)], own.at[h, part], own_sem.at[h, part]
        )
        for h in range(KVH)
        for part in range(2)
    ]
    q_loads, g_loads = [], []
    for h in range(KVH):
        cols = pl.ds(h * MEMBERS * HD, MEMBERS * HD)
        q_loads.append(pltpu.make_async_copy(q_hbm.at[0, :, cols], q_v.at[:, cols], q_sem.at[h]))
        g_loads.append(pltpu.make_async_copy(g_hbm.at[0, :, cols], g_v.at[:, cols], g_sem.at[h]))
    for load in own_loads + small + [q_loads[0], g_loads[0]] + q_loads[1:] + g_loads[1:]:
        load.start()

    def hop(k, h):
        return pltpu.make_async_remote_copy(
            src_ref=own.at[h] if k == 0 else cand.at[k - 1, h],
            dst_ref=cand.at[k, h],
            send_sem=f_send.at[k, h],
            recv_sem=f_recv.at[k, h],
            device_id=(right, grp),
            device_id_type=MESH,
        )

    def pump(k, h):
        hop(k - 1, h).wait_recv()
        hop(k, h).start()

    left2 = lax.rem(me + ZS * YS - 2, ZS * YS)

    def back(k, h):
        target = left2 if k == 1 and h >= LATE else left
        return pltpu.make_async_remote_copy(
            src_ref=gsend.at[k, h],
            dst_ref=grecv.at[k, h],
            send_sem=b_send.at[k, h],
            recv_sem=b_recv.at[k, h],
            device_id=(target, grp),
            device_id_type=MESH,
        )

    def back_step(k, h):
        back(k + 1, h).wait_recv()
        gsend[k, h] = (parts[k + 1, h] + grecv[k + 1, h].astype(F32)).astype(BF16)
        back(k, h).start()

    def exchange(buf, mine, order, peer_of, send_sem, recv_sem):
        def copy(j, slot):
            return pltpu.make_async_remote_copy(
                src_ref=buf.at[slot],
                dst_ref=buf.at[slot],
                send_sem=send_sem.at[j],
                recv_sem=recv_sem,
                device_id=peer_of(j),
                device_id_type=MESH,
            )

        def go(value):
            buf[mine] = value
            for j in order:
                copy(j, mine).start()

        def finish():
            others = buf.at[pl.ds(0, len(order))]
            pltpu.make_async_copy(others, others, recv_sem).wait()
            return jnp.sum(buf[...], axis=0)

        def drain():
            for j in order:
                copy(j, mine).wait_send()

        return go, finish, drain

    go1, end1, drain1 = exchange(
        ar1, my_y * GS + grp, plane_order, plane_peer, a1_send, a1_recv
    )
    go2, end2, drain2 = exchange(ar2, my_z, z_order, z_peer, a2_send, a2_recv)

    for load in own_loads:
        load.wait()
    pl.semaphore_wait(barrier, len(partners))
    for h in range(KVH):
        hop(0, h).start()
    tell(0)

    key_at = lax.broadcasted_iota(jnp.int32, (BLK, ROWS), 0)
    row_at = lax.rem(lax.broadcasted_iota(jnp.int32, (BLK, ROWS), 1), BLK)
    tri = key_at <= row_at
    ones8 = jnp.ones((8, HD), BF16)
    sub16 = lax.broadcasted_iota(jnp.int32, (16, ROWS), 0)
    wide16 = jnp.concatenate(
        [
            jnp.zeros((16, HD), BF16),
            jnp.where(lax.broadcasted_iota(jnp.int32, (16, HD), 0) < 2, 1.0, 0.0).astype(BF16),
        ],
        axis=1,
    )
    for load in small:
        load.wait()
    cq = qgain[...]
    ck = kgain[...]
    cqk = cq * ck
    slots = (me - owner[0, 0], me - owner[0, 1])
    same = jnp.where((start[0, 1] == 1) | (owner[0, 0] != owner[0, 1]), 0.0, 1.0).astype(F32)

    def rows_of(ref, n, h):
        return jnp.concatenate(
            [
                ref[n * BLK : (n + 1) * BLK, (h * MEMBERS + m) * HD : (h * MEMBERS + m + 1) * HD]
                for m in range(MEMBERS)
            ],
            axis=0,
        )

    def local_keys(h):
        raw = kv_v[:, h * HD : (h + 1) * HD].astype(F32)
        inverse = unit_factor(raw)
        return raw, inverse, raw * inverse * cqk

    def over_keys(a):
        return jnp.sum(a, axis=0, keepdims=True)

    stats = {}

    def before(h):
        q_loads[h].wait()
        g_loads[h].wait()
        k_b = local_keys(h)[2].astype(BF16)
        v_b = kv_v[:, KW + h * HD : KW + (h + 1) * HD]
        for n in range(2):
            count = (n + 1) * BLK
            at = n * BLK
            x = rows_of(q_v, n, h)
            g = rows_of(g_v, n, h)
            s = lax.rsqrt(nt(ones8, x * x)[0:1] * (1.0 / HD) + NORM_EPS)
            raw = nt(k_b[:count], x)
            e = jnp.exp2(raw * (s * (SCALE * LOG2E)))
            if n == 0:
                e = jnp.where(tri, e, 0.0)
            else:
                e = jnp.concatenate([e[:BLK] * same, jnp.where(tri, e[BLK:], 0.0)], axis=0)
            d = nt(v_b[:count], g)
            e_v[h, at : at + count] = e
            d_v[h, at : at + count] = d
            er = e * raw
            stats[h, n] = (s, over_keys(e), over_keys(e * d), over_keys(er), over_keys(er * d))

    def pick(slot, h, part):
        mine = own[h, part].astype(F32)
        got = [cand[k, h, part].astype(F32) for k in range(SPAN - 1)]
        return jnp.where(
            slot == 0, mine, jnp.where(slot == 1, got[0], jnp.where(slot == 2, got[1], got[2]))
        )

    kept = {}

    def middle(h):
        hop(SPAN - 2, h).wait_recv()
        full_l = local_keys(h)[2]
        k_b = full_l.astype(BF16)
        dks, d_p = [], []
        total = jnp.zeros((8, HD), F32)
        for n in range(2):
            count = (n + 1) * BLK
            at = n * BLK
            praw = pick(slots[n], h, 0)
            full = praw * unit_factor(praw) * cqk
            p_b = full.astype(BF16)
            w_b = pick(slots[n], h, 1).astype(BF16)
            x = rows_of(q_v, n, h)
            g = rows_of(g_v, n, h)
            s, t, u, xs, ws = stats[h, n]
            raw = nt(p_b, x)
            e_p = jnp.exp2(raw * (s * (SCALE * LOG2E)))
            d_prob = nt(w_b, g)
            inv = 1.0 / (t + over_keys(e_p))
            e_d = e_p * d_prob
            er = e_p * raw
            delta = (u + over_keys(e_d)) * inv
            m = (ws + over_keys(er * d_prob) - delta * (xs + over_keys(er))) * inv
            r = s * SCALE
            prob_l = e_v[h, at : at + count] * inv
            prob_p = e_p * inv
            d2 = jnp.concatenate(
                [
                    (prob_l * ((d_v[h, at : at + count] - delta) * r)).astype(BF16),
                    (prob_p * ((d_prob - delta) * r)).astype(BF16),
                ],
                axis=0,
            )
            prob = jnp.concatenate([prob_l.astype(BF16), prob_p.astype(BF16)], axis=0)
            dk = nn(d2, x)
            if h >= LATE:
                prob_v[h - LATE, n, : count + BLK] = prob
            else:
                kept["prob", n] = prob
            fac = s * s * s * m * (SCALE / HD)
            hi = fac.astype(BF16).astype(F32)
            extra = jnp.where(sub16 == 0, hi, jnp.where(sub16 == 1, fac - hi, 0.0)).astype(BF16)
            lhs_v[h, n, : count + BLK] = d2
            lhs_v[h, n, count + BLK : count + BLK + 16] = extra
            kept[h, n] = jnp.concatenate([k_b[:count], p_b], axis=0)
            d_p.append(cq * dk[count:])
            dks.append(dk[:count])
            total += fold8(full * dk[count:])
        for k in range(SPAN):
            term = jnp.where(slots[0] == k, d_p[0], 0.0) + jnp.where(slots[1] == k, d_p[1], 0.0)
            put_part(k, h, 0, term)
        dk = jnp.concatenate([dks[0] + dks[1][:BLK], dks[1][BLK:]], axis=0)
        kept[h] = dk
        return total + fold8(full_l * dk)

    def put_part(k, h, part, term):
        if k == SPAN - 1 or (k == 1 and h >= LATE):
            gsend[k - 1, h, part] = term.astype(BF16)
        else:
            parts[k, h, part] = term

    def values(h):
        dvs, d_p = [], []
        for n in range(2):
            count = (n + 1) * BLK
            prob = prob_v[h - LATE, n, : count + BLK] if h >= LATE else kept["prob", n]
            dv = nn(prob, rows_of(g_v, n, h))
            dvs.append(dv[:count])
            d_p.append(dv[count:])
        for k in range(SPAN):
            term = jnp.where(slots[0] == k, d_p[0], 0.0) + jnp.where(slots[1] == k, d_p[1], 0.0)
            put_part(k, h, 1, term)
        back(SPAN - 2, h).start()
        if h >= LATE:
            back(0, h).start()
        dv = jnp.concatenate([dvs[0] + dvs[1][:BLK], dvs[1][BLK:]], axis=0)
        kvg_v[0, :, KW + h * HD : KW + (h + 1) * HD] = dv.astype(BF16)

    def after(h):
        raw_l, inverse, _ = local_keys(h)
        kvg_v[0, :, h * HD : (h + 1) * HD] = norm_backward(raw_l, inverse, cqk * kept[h]).astype(BF16)
        for n in range(2):
            count = (n + 2) * BLK
            rhs = jnp.concatenate(
                [jnp.concatenate([kept[h, n], jnp.zeros((count, HD), BF16)], axis=1), wide16], axis=0
            )
            z = tn(lhs_v[h, n, : count + 16], rhs)
            x = rows_of(q_v, n, h).astype(F32)
            dx = (z[:, :HD] - x * z[:, HD:]).astype(BF16)
            for m in range(MEMBERS):
                c = (h * MEMBERS + m) * HD
                qg_v[0, n * BLK : (n + 1) * BLK, c : c + HD] = dx[m * BLK : (m + 1) * BLK]

    before(0)
    hear(0)
    tell(1)
    before(1)
    before(2)
    pump(1, 0)
    pump(1, 1)
    hear(1)
    tell(2)
    pump(1, 2)
    pump(1, 3)
    before(3)
    for h in range(KVH):
        pump(2, h)
    total = middle(0)
    values(0)
    total += middle(1)
    values(1)
    total += middle(2)
    values(2)
    total += middle(3)
    hear(2)
    go1(jnp.sum(total, axis=0, keepdims=True))
    values(3)
    back_step(1, 0)
    back_step(1, 1)
    after(0)
    back_step(1, 2)
    after(1)
    go2(end1())
    back_step(1, 3)
    back_step(0, 0)
    back_step(0, 1)
    after(2)
    after(3)

    def finish_prompt(h):
        back(0, h).wait_recv()
        both = parts[0, h] + grecv[0, h].astype(F32)
        if h >= LATE:
            back(1, h).wait_recv()
            both = both + grecv[1, h].astype(F32)
        raw = own[h, 0].astype(F32)
        pg_v[0, :, h * HD : (h + 1) * HD] = norm_backward(raw, unit_factor(raw), ck * both[0]).astype(BF16)
        pg_v[0, :, KW + h * HD : KW + (h + 1) * HD] = both[1].astype(BF16)

    for h in range(KVH):
        finish_prompt(h)
    for k in range(SPAN - 1):
        for h in range(KVH):
            hop(k, h).wait_send()
            back(k, h).wait_send()
    drain1()
    summed = end2() * (1.0 / math.sqrt(GS * ZS * YS * CT))
    gains_ref[0:1] = summed / cq
    gains_ref[1:2] = summed / ck
    drain2()


def shards(queries, out_grad, keys_values, prompt_kv, q_gain, k_gain, block_owner, block_start):
    hbm = pl.BlockSpec(memory_space=pltpu.HBM)
    anywhere = pl.BlockSpec(memory_space=pl.ANY)
    vmem = pl.BlockSpec(memory_space=pltpu.VMEM)
    dma = pltpu.SemaphoreType.DMA
    held = pl.pallas_call(
        kernel,
        out_shape=(
            pltpu.VMEM((1, CT, QW), BF16),
            pltpu.VMEM((1, CT, 2 * KW), BF16),
            pltpu.VMEM((1, P_SIZE, 2 * KW), BF16),
            pltpu.VMEM((2, HD), F32),
        ),
        in_specs=[hbm] * 8,
        out_specs=(vmem, vmem, vmem, vmem),
        scratch_shapes=[
            pltpu.VMEM((CT, QW), BF16),
            pltpu.VMEM((CT, QW), BF16),
            pltpu.VMEM((CT, 2 * KW), BF16),
            pltpu.VMEM((KVH, 2, P_SIZE, HD), BF16),
            pltpu.VMEM((1, HD), F32),
            pltpu.VMEM((1, HD), F32),
            pltpu.SMEM((1, 2), jnp.int32),
            pltpu.SMEM((1, 2), jnp.int32),
            pltpu.VMEM((KVH, 3 * BLK, ROWS), F32),
            pltpu.VMEM((KVH, 3 * BLK, ROWS), F32),
            pltpu.VMEM((KVH, 2, 3 * BLK + 16, ROWS), BF16),
            pltpu.VMEM((SPAN - 1, KVH, 2, P_SIZE, HD), BF16),
            pltpu.VMEM((SPAN - 1, KVH, 2, P_SIZE, HD), F32),
            pltpu.VMEM((SPAN - 1, KVH, 2, P_SIZE, HD), BF16),
            pltpu.VMEM((SPAN - 1, KVH, 2, P_SIZE, HD), BF16),
            pltpu.VMEM((KVH - LATE, 2, 3 * BLK, ROWS), BF16),
            pltpu.VMEM((YS * GS, 1, HD), F32),
            pltpu.VMEM((ZS, 1, HD), F32),
            dma((KVH,)),
            dma((KVH,)),
            dma((5,)),
            dma((KVH, 2)),
            dma((SPAN - 1, KVH)),
            dma((SPAN - 1, KVH)),
            dma((SPAN - 1, KVH)),
            dma((SPAN - 1, KVH)),
            dma((YS * GS,)),
            dma,
            dma((ZS,)),
            dma,
            pltpu.SemaphoreType.REGULAR((3,)),
        ],
        compiler_params=pltpu.CompilerParams(
            collective_id=0, has_side_effects=True, vmem_limit_bytes=60 * 1024 * 1024
        ),
        name="prefix_attention_grad",
    )(
        queries,
        out_grad,
        keys_values,
        prompt_kv,
        q_gain.reshape(1, HD),
        k_gain.reshape(1, HD),
        block_owner,
        block_start,
    )
    return pl.pallas_call(
        hand_over,
        out_shape=tuple(jax.ShapeDtypeStruct(a.shape, a.dtype) for a in held),
        in_specs=[vmem] * 4,
        out_specs=(anywhere,) * 4,
        scratch_shapes=[dma((KVH * 2 + 3,))],
        compiler_params=pltpu.CompilerParams(vmem_limit_bytes=8 * 1024 * 1024),
        name="hand_over",
    )(*held)


def hand_over(qg, kvg, pg, gains, qg_out, kvg_out, pg_out, gains_out, sem):
    copies = []
    for i in range(2 * KVH):
        rows = pl.ds(i * 16, 16)
        copies.append(pltpu.make_async_copy(qg.at[0, rows], qg_out.at[0, rows], sem.at[i]))
    copies.append(pltpu.make_async_copy(kvg, kvg_out, sem.at[2 * KVH]))
    copies.append(pltpu.make_async_copy(pg, pg_out, sem.at[2 * KVH + 1]))
    copies.append(pltpu.make_async_copy(gains, gains_out, sem.at[2 * KVH + 2]))
    for copy in copies:
        copy.start()
    for copy in copies:
        copy.wait()


def solution(mesh):
    placed = (
        P("group", "dp", None),
        P("group", "dp", None),
        P("group", "dp", None),
        P("group", "dp", None),
        P(),
        P(),
        P("group", "dp"),
        P("group", "dp"),
    )
    return jax.shard_map(
        shards,
        mesh=mesh,
        in_specs=placed,
        out_specs=(P("group", "dp", None), P("group", "dp", None), P("group", "dp", None), P()),
        check_vma=False,
    )
```

```python
import functools
import math

import jax
import jax.numpy as jnp
from jax import lax
from jax.experimental import pallas as pl
from jax.experimental.pallas import tpu as pltpu
from jax.sharding import PartitionSpec as P

H = 32
KVH = 4
HD = 128
BLK = 64
SPAN = 4
P_SIZE = 64
QW = 4096
KW = 512
CT = 128
MEMBERS = H // KVH
ROWS = MEMBERS * BLK
NORM_EPS = 1e-06
SCALE = HD**-0.5
LOG2E = math.log2(math.e)
LATE = 2
ZS = 16
YS = 4
GS = 8
F32 = jnp.float32
BF16 = jnp.bfloat16
MESH = pl.DeviceIdType.MESH


def nt(a, b):
    return lax.dot_general(a, b, (((1,), (1,)), ((), ())), preferred_element_type=F32)


def nn(a, b):
    return jnp.dot(a, b, preferred_element_type=F32)


def tn(a, b):
    return lax.dot_general(a, b, (((0,), (0,)), ((), ())), preferred_element_type=F32)


def fold8(a):
    return jnp.sum(a.reshape(a.shape[0] // 8, 8, a.shape[1]), axis=0)


def unit_factor(raw):
    return lax.rsqrt(jnp.mean(raw * raw, axis=-1, keepdims=True) + NORM_EPS)


def norm_backward(raw, inverse, weighted):
    return inverse * weighted - raw * (inverse * inverse * inverse) * jnp.mean(
        raw * weighted, axis=-1, keepdims=True
    )


def kernel(
    q_hbm, g_hbm, kv_hbm, p_hbm, qgain_hbm, kgain_hbm, owner_hbm, start_hbm,
    qg_v, kvg_v, pg_v, gains_ref,
    q_v, g_v, kv_v, own, own_raw, qgain, kgain, owner, start,
    e_v, d_v, lhs_v, cand, parts, gsend, grecv, prob_v, ar1, ar2,
    q_sem, g_sem, small_sem, own_sem, f_send, f_recv, b_send, b_recv,
    a1_send, a1_recv, a2_send, a2_recv, known,
):
    me = lax.axis_index("dp")
    grp = lax.axis_index("group")
    right, left = lax.rem(me + 1, ZS * YS), lax.rem(me + ZS * YS - 1, ZS * YS)
    my_y, my_z = me // ZS, lax.rem(me, ZS)

    def plane_at(j):
        return lax.rem(my_y + j // GS, YS), lax.rem(grp + j % GS, GS)

    def plane_peer(j):
        y, g = plane_at(j)
        return (y * ZS + my_z, g)

    def z_peer(j):
        return (my_y * ZS + lax.rem(my_z + j, ZS), grp)

    def ring_steps(j, size):
        return min(j, size - j)

    plane_order = sorted(
        range(1, YS * GS),
        key=lambda j: -ring_steps(j // GS, YS) - ring_steps((j % GS + 1) // 2, GS // 2),
    )
    z_order = sorted(range(1, ZS), key=lambda j: -ring_steps(j, ZS))

    def x_peer(j):
        return (me, lax.rem(grp + 2 * j, GS))

    def y_peer(j):
        return (lax.rem(my_y + j, YS) * ZS + my_z, grp)

    other_core = (me, grp + 1 - 2 * lax.rem(grp, 2))
    beside = [y_peer(1), y_peer(YS - 1), x_peer(1), x_peer(GS // 2 - 1), other_core]
    rounds = [
        beside + [z_peer(1), z_peer(ZS - 1)],
        beside + [y_peer(2), x_peer(2), z_peer(2), z_peer(ZS - 2)],
        [other_core, z_peer(4), z_peer(ZS - 4)],
    ]

    def tell(i):
        for peer in rounds[i]:
            pl.semaphore_signal(known.at[i], inc=1, device_id=peer, device_id_type=MESH)

    def hear(i):
        pl.semaphore_wait(known.at[i], len(rounds[i]))

    barrier = pltpu.get_barrier_semaphore()
    partners = [(right, grp), (left, grp)] + rounds[0]
    for peer in partners:
        pl.semaphore_signal(barrier, inc=1, device_id=peer, device_id_type=MESH)

    small = [
        pltpu.make_async_copy(src, dst, small_sem.at[i])
        for i, (src, dst) in enumerate(
            [
                (kv_hbm.at[0], kv_v),
                (qgain_hbm, qgain),
                (kgain_hbm, kgain),
                (owner_hbm, owner),
                (start_hbm, start),
            ]
        )
    ]
    own_loads = [
        pltpu.make_async_copy(
            p_hbm.at[0, :, pl.ds(part * KW + h * HD, HD)], own.at[h, part], own_sem.at[h, part]
        )
        for h in range(KVH)
        for part in range(2)
    ]
    q_loads, g_loads = [], []
    for h in range(KVH):
        cols = pl.ds(h * MEMBERS * HD, MEMBERS * HD)
        q_loads.append(pltpu.make_async_copy(q_hbm.at[0, :, cols], q_v.at[:, cols], q_sem.at[h]))
        g_loads.append(pltpu.make_async_copy(g_hbm.at[0, :, cols], g_v.at[:, cols], g_sem.at[h]))
    for load in own_loads + small + [q_loads[0], g_loads[0]] + q_loads[1:] + g_loads[1:]:
        load.start()

    def hop(k, h):
        return pltpu.make_async_remote_copy(
            src_ref=own.at[h] if k == 0 else cand.at[k - 1, h],
            dst_ref=cand.at[k, h],
            send_sem=f_send.at[k, h],
            recv_sem=f_recv.at[k, h],
            device_id=(right, grp),
            device_id_type=MESH,
        )

    def pump(k, h):
        hop(k - 1, h).wait_recv()
        hop(k, h).start()

    left2 = lax.rem(me + ZS * YS - 2, ZS * YS)

    def back(k, h):
        target = left2 if k == 1 and h >= LATE else left
        return pltpu.make_async_remote_copy(
            src_ref=gsend.at[k, h],
            dst_ref=grecv.at[k, h],
            send_sem=b_send.at[k, h],
            recv_sem=b_recv.at[k, h],
            device_id=(target, grp),
            device_id_type=MESH,
        )

    def back_step(k, h):
        back(k + 1, h).wait_recv()
        gsend[k, h] = (parts[k + 1, h] + grecv[k + 1, h].astype(F32)).astype(BF16)
        back(k, h).start()

    def exchange(buf, mine, order, peer_of, send_sem, recv_sem):
        def copy(j, slot):
            return pltpu.make_async_remote_copy(
                src_ref=buf.at[slot],
                dst_ref=buf.at[slot],
                send_sem=send_sem.at[j],
                recv_sem=recv_sem,
                device_id=peer_of(j),
                device_id_type=MESH,
            )

        def go(value):
            buf[mine] = value
            for j in order:
                copy(j, mine).start()

        def finish():
            others = buf.at[pl.ds(0, len(order))]
            pltpu.make_async_copy(others, others, recv_sem).wait()
            return jnp.sum(buf[...], axis=0)

        def drain():
            for j in order:
                copy(j, mine).wait_send()

        return go, finish, drain

    go1, end1, drain1 = exchange(
        ar1, my_y * GS + grp, plane_order, plane_peer, a1_send, a1_recv
    )
    go2, end2, drain2 = exchange(ar2, my_z, z_order, z_peer, a2_send, a2_recv)

    for load in own_loads:
        load.wait()
    small[1].wait()
    small[2].wait()
    cq = qgain[...]
    ck = kgain[...]
    cqk = cq * ck
    for h in range(KVH):
        raw = own[h, 0].astype(F32)
        own_raw[h] = own[h, 0]
        own[h, 0] = (raw * unit_factor(raw) * cqk).astype(BF16)
        if h == 0:
            pl.semaphore_wait(barrier, len(partners))
        hop(0, h).start()
    tell(0)

    key_at = lax.broadcasted_iota(jnp.int32, (BLK, ROWS), 0)
    row_at = lax.rem(lax.broadcasted_iota(jnp.int32, (BLK, ROWS), 1), BLK)
    tri = key_at <= row_at
    ones8 = jnp.ones((8, HD), BF16)
    sub16 = lax.broadcasted_iota(jnp.int32, (16, ROWS), 0)
    wide16 = jnp.concatenate(
        [
            jnp.zeros((16, HD), BF16),
            jnp.where(lax.broadcasted_iota(jnp.int32, (16, HD), 0) < 2, 1.0, 0.0).astype(BF16),
        ],
        axis=1,
    )
    for load in small[:1] + small[3:]:
        load.wait()
    slots = (me - owner[0, 0], me - owner[0, 1])
    same = jnp.where((start[0, 1] == 1) | (owner[0, 0] != owner[0, 1]), 0.0, 1.0).astype(F32)

    def rows_of(ref, n, h):
        return jnp.concatenate(
            [
                ref[n * BLK : (n + 1) * BLK, (h * MEMBERS + m) * HD : (h * MEMBERS + m + 1) * HD]
                for m in range(MEMBERS)
            ],
            axis=0,
        )

    def local_keys(h):
        raw = kv_v[:, h * HD : (h + 1) * HD].astype(F32)
        inverse = unit_factor(raw)
        return raw, inverse, raw * inverse * cqk

    def over_keys(a):
        return jnp.sum(a, axis=0, keepdims=True)

    stats = {}

    def before(h):
        q_loads[h].wait()
        g_loads[h].wait()
        k_b = local_keys(h)[2].astype(BF16)
        v_b = kv_v[:, KW + h * HD : KW + (h + 1) * HD]
        for n in range(2):
            count = (n + 1) * BLK
            at = n * BLK
            x = rows_of(q_v, n, h)
            g = rows_of(g_v, n, h)
            s = lax.rsqrt(nt(ones8, x * x)[0:1] * (1.0 / HD) + NORM_EPS)
            raw = nt(k_b[:count], x)
            e = jnp.exp2(raw * (s * (SCALE * LOG2E)))
            if n == 0:
                e = jnp.where(tri, e, 0.0)
            else:
                e = jnp.concatenate([e[:BLK] * same, jnp.where(tri, e[BLK:], 0.0)], axis=0)
            d = nt(v_b[:count], g)
            e_v[h, at : at + count] = e
            d_v[h, at : at + count] = d
            er = e * raw
            stats[h, n] = (s, over_keys(e), over_keys(e * d), over_keys(er), over_keys(er * d))

    def pick(slot, h, part):
        mine = own[h, part].astype(F32)
        got = [cand[k, h, part].astype(F32) for k in range(SPAN - 1)]
        return jnp.where(
            slot == 0, mine, jnp.where(slot == 1, got[0], jnp.where(slot == 2, got[1], got[2]))
        )

    kept = {}

    def middle(h):
        hop(SPAN - 2, h).wait_recv()
        full_l = local_keys(h)[2]
        k_b = full_l.astype(BF16)
        dks, d_p = [], []
        total = jnp.zeros((8, HD), F32)
        for n in range(2):
            count = (n + 1) * BLK
            at = n * BLK
            p_b = pick(slots[n], h, 0).astype(BF16)
            w_b = pick(slots[n], h, 1).astype(BF16)
            x = rows_of(q_v, n, h)
            g = rows_of(g_v, n, h)
            s, t, u, xs, ws = stats[h, n]
            raw = nt(p_b, x)
            e_p = jnp.exp2(raw * (s * (SCALE * LOG2E)))
            d_prob = nt(w_b, g)
            inv = 1.0 / (t + over_keys(e_p))
            e_d = e_p * d_prob
            er = e_p * raw
            delta = (u + over_keys(e_d)) * inv
            m = (ws + over_keys(er * d_prob) - delta * (xs + over_keys(er))) * inv
            r = s * SCALE
            prob_l = e_v[h, at : at + count] * inv
            prob_p = e_p * inv
            d2 = jnp.concatenate(
                [
                    (prob_l * ((d_v[h, at : at + count] - delta) * r)).astype(BF16),
                    (prob_p * ((d_prob - delta) * r)).astype(BF16),
                ],
                axis=0,
            )
            prob = jnp.concatenate([prob_l.astype(BF16), prob_p.astype(BF16)], axis=0)
            dk = nn(d2, x)
            if h >= LATE:
                prob_v[h - LATE, n, : count + BLK] = prob
            else:
                kept["prob", n] = prob
            fac = s * s * s * m * (SCALE / HD)
            hi = fac.astype(BF16).astype(F32)
            extra = jnp.where(sub16 == 0, hi, jnp.where(sub16 == 1, fac - hi, 0.0)).astype(BF16)
            lhs_v[h, n, : count + BLK] = d2
            lhs_v[h, n, count + BLK : count + BLK + 16] = extra
            kept[h, n] = jnp.concatenate([k_b[:count], p_b], axis=0)
            d_p.append(cq * dk[count:])
            dks.append(dk[:count])
            total += fold8(p_b.astype(F32) * dk[count:])
        for k in range(SPAN):
            term = jnp.where(slots[0] == k, d_p[0], 0.0) + jnp.where(slots[1] == k, d_p[1], 0.0)
            put_part(k, h, 0, term)
        dk = jnp.concatenate([dks[0] + dks[1][:BLK], dks[1][BLK:]], axis=0)
        kept[h] = dk
        return total + fold8(full_l * dk)

    def put_part(k, h, part, term):
        if k == SPAN - 1 or (k == 1 and h >= LATE):
            gsend[k - 1, h, part] = term.astype(BF16)
        else:
            parts[k, h, part] = term

    def values(h):
        dvs, d_p = [], []
        for n in range(2):
            count = (n + 1) * BLK
            prob = prob_v[h - LATE, n, : count + BLK] if h >= LATE else kept["prob", n]
            dv = nn(prob, rows_of(g_v, n, h))
            dvs.append(dv[:count])
            d_p.append(dv[count:])
        for k in range(SPAN):
            term = jnp.where(slots[0] == k, d_p[0], 0.0) + jnp.where(slots[1] == k, d_p[1], 0.0)
            put_part(k, h, 1, term)
        back(SPAN - 2, h).start()
        if h >= LATE:
            back(0, h).start()
        dv = jnp.concatenate([dvs[0] + dvs[1][:BLK], dvs[1][BLK:]], axis=0)
        kvg_v[0, :, KW + h * HD : KW + (h + 1) * HD] = dv.astype(BF16)

    def after(h):
        raw_l, inverse, _ = local_keys(h)
        kvg_v[0, :, h * HD : (h + 1) * HD] = norm_backward(raw_l, inverse, cqk * kept[h]).astype(BF16)
        for n in range(2):
            count = (n + 2) * BLK
            rhs = jnp.concatenate(
                [jnp.concatenate([kept[h, n], jnp.zeros((count, HD), BF16)], axis=1), wide16], axis=0
            )
            z = tn(lhs_v[h, n, : count + 16], rhs)
            x = rows_of(q_v, n, h).astype(F32)
            dx = (z[:, :HD] - x * z[:, HD:]).astype(BF16)
            for m in range(MEMBERS):
                c = (h * MEMBERS + m) * HD
                qg_v[0, n * BLK : (n + 1) * BLK, c : c + HD] = dx[m * BLK : (m + 1) * BLK]

    before(0)
    hear(0)
    tell(1)
    before(1)
    before(2)
    pump(1, 0)
    pump(1, 1)
    hear(1)
    tell(2)
    pump(1, 2)
    pump(1, 3)
    before(3)
    for h in range(KVH):
        pump(2, h)
    total = middle(0)
    values(0)
    total += middle(1)
    values(1)
    total += middle(2)
    values(2)
    total += middle(3)
    hear(2)
    go1(jnp.sum(total, axis=0, keepdims=True))
    values(3)
    back_step(1, 0)
    back_step(1, 1)
    after(0)
    back_step(1, 2)
    after(1)
    go2(end1())
    back_step(1, 3)
    back_step(0, 0)
    back_step(0, 1)
    after(2)
    after(3)

    def finish_prompt(h):
        back(0, h).wait_recv()
        both = parts[0, h] + grecv[0, h].astype(F32)
        if h >= LATE:
            back(1, h).wait_recv()
            both = both + grecv[1, h].astype(F32)
        raw = own_raw[h].astype(F32)
        pg_v[0, :, h * HD : (h + 1) * HD] = norm_backward(raw, unit_factor(raw), ck * both[0]).astype(BF16)
        pg_v[0, :, KW + h * HD : KW + (h + 1) * HD] = both[1].astype(BF16)

    for h in range(KVH):
        finish_prompt(h)
    for k in range(SPAN - 1):
        for h in range(KVH):
            hop(k, h).wait_send()
            back(k, h).wait_send()
    drain1()
    summed = end2() * (1.0 / math.sqrt(GS * ZS * YS * CT))
    gains_ref[0:1] = summed / cq
    gains_ref[1:2] = summed / ck
    drain2()


def shards(queries, out_grad, keys_values, prompt_kv, q_gain, k_gain, block_owner, block_start):
    hbm = pl.BlockSpec(memory_space=pltpu.HBM)
    anywhere = pl.BlockSpec(memory_space=pl.ANY)
    vmem = pl.BlockSpec(memory_space=pltpu.VMEM)
    dma = pltpu.SemaphoreType.DMA
    held = pl.pallas_call(
        kernel,
        out_shape=(
            pltpu.VMEM((1, CT, QW), BF16),
            pltpu.VMEM((1, CT, 2 * KW), BF16),
            pltpu.VMEM((1, P_SIZE, 2 * KW), BF16),
            pltpu.VMEM((2, HD), F32),
        ),
        in_specs=[hbm] * 8,
        out_specs=(vmem, vmem, vmem, vmem),
        scratch_shapes=[
            pltpu.VMEM((CT, QW), BF16),
            pltpu.VMEM((CT, QW), BF16),
            pltpu.VMEM((CT, 2 * KW), BF16),
            pltpu.VMEM((KVH, 2, P_SIZE, HD), BF16),
            pltpu.VMEM((KVH, P_SIZE, HD), BF16),
            pltpu.VMEM((1, HD), F32),
            pltpu.VMEM((1, HD), F32),
            pltpu.SMEM((1, 2), jnp.int32),
            pltpu.SMEM((1, 2), jnp.int32),
            pltpu.VMEM((KVH, 3 * BLK, ROWS), F32),
            pltpu.VMEM((KVH, 3 * BLK, ROWS), F32),
            pltpu.VMEM((KVH, 2, 3 * BLK + 16, ROWS), BF16),
            pltpu.VMEM((SPAN - 1, KVH, 2, P_SIZE, HD), BF16),
            pltpu.VMEM((SPAN - 1, KVH, 2, P_SIZE, HD), F32),
            pltpu.VMEM((SPAN - 1, KVH, 2, P_SIZE, HD), BF16),
            pltpu.VMEM((SPAN - 1, KVH, 2, P_SIZE, HD), BF16),
            pltpu.VMEM((KVH - LATE, 2, 3 * BLK, ROWS), BF16),
            pltpu.VMEM((YS * GS, 1, HD), F32),
            pltpu.VMEM((ZS, 1, HD), F32),
            dma((KVH,)),
            dma((KVH,)),
            dma((5,)),
            dma((KVH, 2)),
            dma((SPAN - 1, KVH)),
            dma((SPAN - 1, KVH)),
            dma((SPAN - 1, KVH)),
            dma((SPAN - 1, KVH)),
            dma((YS * GS,)),
            dma,
            dma((ZS,)),
            dma,
            pltpu.SemaphoreType.REGULAR((3,)),
        ],
        compiler_params=pltpu.CompilerParams(
            collective_id=0, has_side_effects=True, vmem_limit_bytes=60 * 1024 * 1024
        ),
        name="prefix_attention_grad",
    )(
        queries,
        out_grad,
        keys_values,
        prompt_kv,
        q_gain.reshape(1, HD),
        k_gain.reshape(1, HD),
        block_owner,
        block_start,
    )
    return pl.pallas_call(
        hand_over,
        out_shape=tuple(jax.ShapeDtypeStruct(a.shape, a.dtype) for a in held),
        in_specs=[vmem] * 4,
        out_specs=(anywhere,) * 4,
        scratch_shapes=[dma((4,))],
        compiler_params=pltpu.CompilerParams(vmem_limit_bytes=8 * 1024 * 1024),
        name="hand_over",
    )(*held)


def hand_over(qg, kvg, pg, gains, qg_out, kvg_out, pg_out, gains_out, sem):
    pairs = [(qg, qg_out), (kvg, kvg_out), (pg, pg_out), (gains, gains_out)]
    copies = [pltpu.make_async_copy(src, dst, sem.at[i]) for i, (src, dst) in enumerate(pairs)]
    for copy in copies:
        copy.start()
    for copy in copies:
        copy.wait()


def solution(mesh):
    placed = (
        P("group", "dp", None),
        P("group", "dp", None),
        P("group", "dp", None),
        P("group", "dp", None),
        P(),
        P(),
        P("group", "dp"),
        P("group", "dp"),
    )
    return jax.shard_map(
        shards,
        mesh=mesh,
        in_specs=placed,
        out_specs=(P("group", "dp", None), P("group", "dp", None), P("group", "dp", None), P()),
        check_vma=False,
    )
```
